256 devices in a mesh: row: 8 (over x, core), col: 16 (over y_lo, z), dp: 2 (over y_hi).
Axes of the slice: x: 4, y: 4 (y_hi: 2, y_lo: 2; y = y_hi * 2 + y_lo), z: 8, core: 2. Of those that a mesh axis runs over, the one named last changes fastest.
Arguments:
- tokens: bfloat16 [1024, 6144], P(('row', 'dp'), 'col'), may hold values from -6 to 6
- grad_out: bfloat16 [1024, 6144], P(('row', 'dp'), 'col'), may hold values from -6 to 6
- w_up: bfloat16 [6144, 24576], P('col', 'row'), may hold values from -0.15625 to 0.15625
- w_down: bfloat16 [24576, 6144], P('row', 'col'), may hold values from -0.078125 to 0.078125
- mask_up: int32 [96, 384], P('col', 'row'), may hold values from 0 to 1, as said below
- mask_down: int32 [384, 96], P('row', 'col'), may hold values from 0 to 1, as said below
Outputs:
- out_act: bfloat16 [1024, 6144], P(('row', 'dp'), 'col')
- grad_in: bfloat16 [1024, 6144], P(('row', 'dp'), 'col')
- grad_w_up: bfloat16 [6144, 24576], P('col', ('row', 'dp'))
- grad_w_down: bfloat16 [24576, 6144], P(('row', 'dp'), 'col')
The draws below stay inside these ranges and needn't reach their ends.
Inputs may be any that keep to these rules, and one draw needn't show every extreme that they name: `mask_up`: 1 marks a live block of 64 x 64 weights, 0 a block that is absent; the share of live blocks varies between regions of 8 x 8 blocks. `mask_down`: 1 marks a live block of 64 x 64 weights, 0 a block that is absent; the share of live blocks varies between regions of 8 x 8 blocks.
All inputs are finite; a program needn't handle non-finite values.
Results may differ from the reference program's by a relative error of at most 0.019.
Values may be sent and summed in bfloat16 or wider, within the bound.
A program may use at most 128 MiB of HBM per device.

```python
import jax
import jax.numpy as jnp
from jax import lax

D = 6144
FF = 24576
BLOCK = 64
TOKENS = 1024


def region_mask(key, row_blocks, col_blocks):
    density_key, cell_key = jax.random.split(key)
    region_rows = (row_blocks + 7) // 8
    region_cols = (col_blocks + 7) // 8
    density = jax.random.randint(density_key, (region_rows, region_cols), 4, 29)
    block_density = jnp.repeat(jnp.repeat(density, 8, axis=0), 8, axis=1)[:row_blocks, :col_blocks]
    cell_draw = jax.random.randint(cell_key, (row_blocks, col_blocks), 0, 64)
    return (cell_draw < block_density).astype(jnp.int32)


def draw_mask_up(key, part):
    key = jax.random.fold_in(key, 11)
    return region_mask(key, D // BLOCK, FF // BLOCK)


def draw_mask_down(key, part):
    key = jax.random.fold_in(key, 23)
    return region_mask(key, FF // BLOCK, D // BLOCK)


def steps_of(stream_key, dims, shards, least, high):
    loudness = 1.0
    for axis_at, shards_of in shards:
        steps = jax.random.uniform(jax.random.fold_in(jax.random.fold_in(stream_key, 6), axis_at), (shards_of,), jnp.float32, least / len(shards), high / len(shards))
        loudness = loudness * jnp.repeat(jnp.exp(steps), dims[axis_at] // shards_of).reshape((-1,) + (1,) * (len(dims) - 1 - axis_at))
    return loudness


def gaussian(own_key, extent, scale, limit, pieces=(), dtype=jnp.bfloat16):
    result = scale * jax.random.normal(own_key, extent, jnp.float32)
    if pieces:
        result = result * steps_of(own_key, extent, pieces, -0.22, 0.18)
    return jnp.clip(result, -limit, limit).astype(dtype)


def setup_inputs(seed: int = 0) -> dict:
    keys = jax.random.split(jax.random.key(seed), 7)
    return {
        "tokens": gaussian(keys[0], (TOKENS, D), 1.0, 6.0, ((0, 16), (1, 16))),
        "grad_out": gaussian(keys[1], (TOKENS, D), 1.0, 6.0, ((0, 16), (1, 16))),
        "w_up": gaussian(keys[2], (D, FF), (D // 4) ** -0.5, 0.15625, ((0, 16), (1, 8))),
        "w_down": gaussian(keys[3], (FF, D), (FF // 4) ** -0.5, 0.078125, ((0, 8), (1, 16))),
        "mask_up": draw_mask_up(jax.random.fold_in(keys[6], 71), 0),
        "mask_down": draw_mask_down(jax.random.fold_in(keys[6], 71), 0),
    }


COEF_ROOT = 0.7978845608028654
COEF_CUBE = 0.044715


def gelu_pair(pre_act):
    argument = COEF_ROOT * (pre_act + COEF_CUBE * pre_act * pre_act * pre_act)
    tangent = jnp.tanh(argument)
    activated = 0.5 * pre_act * (1.0 + tangent)
    gelu_slope = 0.5 * (1.0 + tangent) + 0.5 * pre_act * (1.0 - tangent * tangent) * COEF_ROOT * (1.0 + 3.0 * COEF_CUBE * pre_act * pre_act)
    return activated, gelu_slope


def spread(mask_blocks):
    row_blocks, col_blocks = mask_blocks.shape
    wide = jnp.broadcast_to(mask_blocks.astype(jnp.bfloat16)[:, None, :, None], (row_blocks, BLOCK, col_blocks, BLOCK))
    return wide.reshape(row_blocks * BLOCK, col_blocks * BLOCK)


def times_transposed(left, right):
    return lax.dot_general(left, right, (((1,), (1,)), ((), ())), preferred_element_type=jnp.float32)


def token_contract(left, right):
    return lax.dot_general(left, right, (((0,), (0,)), ((), ())), preferred_element_type=jnp.float32)


def reference(tokens, grad_out, w_up, w_down, mask_up, mask_down):
    up_keep = spread(mask_up)
    down_keep = spread(mask_down)
    up_live = w_up * up_keep
    down_live = w_down * down_keep
    pre_act = jnp.dot(tokens, up_live, preferred_element_type=jnp.float32)
    grad_hidden = times_transposed(grad_out, down_live)
    activated, gelu_slope = gelu_pair(pre_act)
    hidden = activated.astype(jnp.bfloat16)
    grad_pre = (grad_hidden * gelu_slope).astype(jnp.bfloat16)
    out_act = jnp.dot(hidden, down_live, preferred_element_type=jnp.float32).astype(jnp.bfloat16)
    grad_in = times_transposed(grad_pre, up_live).astype(jnp.bfloat16)
    tok_scale = float(TOKENS) ** -0.5
    grad_w_up = (token_contract(tokens, grad_pre) * tok_scale * up_keep.astype(jnp.float32)).astype(jnp.bfloat16)
    grad_w_down = (token_contract(hidden, grad_out) * tok_scale * down_keep.astype(jnp.float32)).astype(jnp.bfloat16)
    return out_act, grad_in, grad_w_up, grad_w_down
```

```python
import jax
import jax.numpy as jnp
from jax import lax
from jax.sharding import PartitionSpec as P

BLOCK = 64


COEF_ROOT = 0.7978845608028654
COEF_CUBE = 0.044715


def gelu_pair(pre_act):
    argument = COEF_ROOT * (pre_act + COEF_CUBE * pre_act * pre_act * pre_act)
    tangent = jnp.tanh(argument)
    activated = 0.5 * pre_act * (1.0 + tangent)
    gelu_slope = 0.5 * (1.0 + tangent) + 0.5 * pre_act * (1.0 - tangent * tangent) * COEF_ROOT * (
        1.0 + 3.0 * COEF_CUBE * pre_act * pre_act
    )
    return (activated, gelu_slope)


def spread(mask_blocks):
    row_blocks, col_blocks = mask_blocks.shape
    wide = jnp.broadcast_to(
        mask_blocks.astype(jnp.bfloat16)[:, None, :, None], (row_blocks, BLOCK, col_blocks, BLOCK)
    )
    return wide.reshape(row_blocks * BLOCK, col_blocks * BLOCK)


def times_transposed(left, right):
    return lax.dot_general(
        left, right, (((1,), (1,)), ((), ())), preferred_element_type=jnp.float32
    )


def token_contract(left, right):
    return lax.dot_general(
        left, right, (((0,), (0,)), ((), ())), preferred_element_type=jnp.float32
    )


def local(tokens, grad_out, w_up, w_down, mask_up, mask_down):
    dp = lax.axis_index("dp")
    half = w_up.shape[1] // 2
    w_up = lax.dynamic_slice_in_dim(w_up, dp * half, half, 1)
    w_down = lax.dynamic_slice_in_dim(w_down, dp * half, half, 0)
    mask_up = lax.dynamic_slice_in_dim(mask_up, dp * (half // BLOCK), half // BLOCK, 1)
    mask_down = lax.dynamic_slice_in_dim(mask_down, dp * (half // BLOCK), half // BLOCK, 0)
    up_keep = spread(mask_up)
    down_keep = spread(mask_down)
    up_live = w_up * up_keep
    down_live = w_down * down_keep
    both = jnp.stack([tokens, grad_out], axis=1)
    both = lax.all_gather(both, ("row", "dp"), axis=0, tiled=True)
    tok_all, grad_all = both[:, 0], both[:, 1]
    pre_part = jnp.dot(tok_all, up_live, preferred_element_type=jnp.float32)
    back_part = times_transposed(grad_all, down_live)
    pre_act = lax.psum_scatter(pre_part.astype(jnp.bfloat16), "col", scatter_dimension=0, tiled=True)
    grad_hidden = lax.psum_scatter(back_part.astype(jnp.bfloat16), "col", scatter_dimension=0, tiled=True)
    activated, slope = gelu_pair(pre_act.astype(jnp.float32))
    hidden = activated.astype(jnp.bfloat16)
    grad_pre = (grad_hidden.astype(jnp.float32) * slope).astype(jnp.bfloat16)
    hidden = lax.all_gather(hidden, "col", axis=0, tiled=True)
    grad_pre = lax.all_gather(grad_pre, "col", axis=0, tiled=True)
    out_part = jnp.dot(hidden, down_live, preferred_element_type=jnp.float32)
    in_part = times_transposed(grad_pre, up_live)
    out_sum = lax.psum_scatter(
        out_part.astype(jnp.bfloat16), ("row", "dp"), scatter_dimension=0, tiled=True
    )
    in_sum = lax.psum_scatter(
        in_part.astype(jnp.bfloat16), ("row", "dp"), scatter_dimension=0, tiled=True
    )
    tok_scale = float(tok_all.shape[0]) ** (-0.5)
    up_grad = token_contract(tok_all, grad_pre) * tok_scale * up_keep.astype(jnp.float32)
    down_grad = token_contract(hidden, grad_all) * tok_scale * down_keep.astype(jnp.float32)
    return (
        out_sum,
        in_sum,
        up_grad.astype(jnp.bfloat16),
        down_grad.astype(jnp.bfloat16),
    )


def solution(mesh):
    in_specs = (
        P(("row", "dp"), "col"),
        P(("row", "dp"), "col"),
        P("col", "row"),
        P("row", "col"),
        P("col", "row"),
        P("row", "col"),
    )
    out_specs = (
        P(("row", "dp"), "col"),
        P(("row", "dp"), "col"),
        P("col", ("row", "dp")),
        P(("row", "dp"), "col"),
    )
    return jax.shard_map(local, mesh=mesh, in_specs=in_specs, out_specs=out_specs, check_vma=False)
```

```python
import jax
import jax.numpy as jnp
from jax import lax
from jax.experimental import pallas as pl
from jax.experimental.pallas import tpu as pltpu
from jax.sharding import PartitionSpec as P

BLOCK = 64
MESH = pl.DeviceIdType.MESH
F32 = jnp.float32
BF16 = jnp.bfloat16

COEF_ROOT = 0.7978845608028654
COEF_CUBE = 0.044715

TOK = 1024
ROWS = 64
DW = 384
D2 = 2 * DW
FQ = 768
C = 3
FC = FQ // C
Z = 8
TB = TOK // Z
MESSAGES = 192


def gelu_pair(pre_act):
    argument = COEF_ROOT * (pre_act + COEF_CUBE * pre_act * pre_act * pre_act)
    tangent = jnp.tanh(argument)
    activated = 0.5 * pre_act * (1.0 + tangent)
    gelu_slope = 0.5 * (1.0 + tangent) + 0.5 * pre_act * (1.0 - tangent * tangent) * COEF_ROOT * (
        1.0 + 3.0 * COEF_CUBE * pre_act * pre_act
    )
    return (activated, gelu_slope)


def dot_nn(a, b):
    return lax.dot_general(a, b, (((1,), (0,)), ((), ())), preferred_element_type=F32)


def dot_nt(a, b):
    return lax.dot_general(a, b, (((1,), (1,)), ((), ())), preferred_element_type=F32)


def dot_tn(a, b):
    return lax.dot_general(a, b, (((0,), (0,)), ((), ())), preferred_element_type=F32)


def kernel(
    tok, grad, wu, wd, ku, kd, out, gin, gwu, gwd,
    stage, x_all, raw_u, raw_un, raw_d, raw_dn, w_u, w_d, snd_u, snd_d,
    part, first, came, hid, acc, core_s, core_r, xs, xr, yfull, ys, yr, fin_s, fin_r,
    gu_s, gu_r, gd_s, gd_r, load_sem, send_sem, recv_sem,
):
    row, col, dp = lax.axis_index("row"), lax.axis_index("col"), lax.axis_index("dp")
    x, core = row // 2, row % 2
    yl, z = col // Z, col % Z
    y = dp * 2 + yl

    def at_y(v):
        v = v % 4
        return {"col": (v % 2) * Z + z, "dp": v // 2}

    def at_x(v):
        return {"row": (v % 4) * 2 + core}

    def at_z(v):
        return {"col": yl * Z + v % Z}

    sibling = {"row": x * 2 + (1 - core)}
    y_next = (at_y(y + 1), at_y(y + 3))
    x_next = (at_x(x + 1), at_x(x + 3))
    z_next = (at_z(z + 1), at_z(z + Z - 1))
    partner = {"col": (1 - yl) * Z + z}

    count = [0]
    sent = []

    def send(src, dst, device):
        at = count[0]
        count[0] += 1
        copy = pltpu.make_async_remote_copy(
            src_ref=src, dst_ref=dst, send_sem=send_sem.at[at], recv_sem=recv_sem.at[at],
            device_id=device, device_id_type=MESH,
        )
        copy.start()
        sent.append(copy)
        return copy

    own_f = pl.multiple_of(y * FQ, FQ)
    near_f = [pl.multiple_of(((y + 1) % 4) * FQ, FQ), pl.multiple_of(((y + 3) % 4) * FQ, FQ)]
    loads = []

    def load(src, dst):
        copy = pltpu.make_async_copy(src, dst, load_sem.at[len(loads)])
        copy.start()
        loads.append(copy)

    for way in range(2):
        load(wu.at[pl.ds(way * 192, 192), pl.ds(near_f[way], FQ)], raw_un.at[way])
        load(wd.at[pl.ds(near_f[way], FQ), :], raw_dn.at[way])
    load(wu.at[:, pl.ds(own_f, FQ)], raw_u)
    load(wd.at[pl.ds(own_f, FQ), :], raw_d)

    barrier = pltpu.get_barrier_semaphore()
    for other in (sibling, *y_next, *x_next, *z_next):
        pl.semaphore_signal(barrier, inc=1, device_id=other, device_id_type=MESH)

    own_rows = pl.multiple_of(row * 128 + dp * ROWS, ROWS)
    stage[0] = tok[...]
    stage[1] = grad[...]
    x_all[core, pl.ds(own_rows, ROWS), 0:DW] = stage[core]
    pl.semaphore_wait(barrier, 7)

    def tok_slice(arr, r, p, half):
        at = pl.multiple_of((x * 2 + r) * 128 + p * ROWS, ROWS)
        return x_all.at[arr, pl.ds(at, ROWS), pl.ds(half * DW, DW)]

    p_of = [((y + 1) % 4) // 2, ((y + 3) % 4) // 2]
    swap = send(
        stage.at[1 - core], x_all.at[1 - core, pl.ds(own_rows, ROWS), pl.ds(0, DW)], sibling
    )
    step_own, step_sib = [], []
    for way in range(2):
        step_own.append(send(tok_slice(core, core, dp, 0), tok_slice(core, core, dp, 1), y_next[way]))
    swap.wait_recv()
    for way in range(2):
        step_sib.append(
            send(tok_slice(core, 1 - core, dp, 0), tok_slice(core, 1 - core, dp, 1), y_next[way])
        )


    weight_in = []
    for copy in loads[:4]:
        copy.wait()
    for c in range(C):
        for way in range(2):
            for i in range(3):
                keep = ku[way * 3 + i : way * 3 + i + 1, pl.ds(near_f[way] + c * FC, FC)]
                snd_u[way, c, i * 64 : i * 64 + 64, :] = (
                    raw_un[way, i * 64 : i * 64 + 64, c * FC : (c + 1) * FC].astype(F32) * keep
                ).astype(BF16)
            for i in range(2):
                at = c * FC + way * 128 + i * 64
                keep = kd[pl.ds(near_f[way] // 64 + at // 64, 1), :]
                snd_d[way, c, i * 64 : i * 64 + 64, :] = (
                    raw_dn[way, at : at + 64, :].astype(F32) * keep
                ).astype(BF16)
        got = []
        for way in range(2):
            got.append(
                send(snd_u.at[way, c], w_u.at[c, pl.ds(DW + way * 192, 192), :], y_next[way])
            )
            got.append(
                send(
                    snd_d.at[way, c],
                    w_d.at[pl.ds(c * FC + way * 128, 128), pl.ds(DW, DW)],
                    y_next[way],
                )
            )
        weight_in.append(got)

    for copy in step_own + step_sib:
        copy.wait_recv()
    before, after = ((y + 3) % 4) // 2, ((y + 1) % 4) // 2
    far = [
        send(tok_slice(core, 0, before, 1), tok_slice(core, 0, before, 0), y_next[0]),
        send(tok_slice(core, 1, after, 1), tok_slice(core, 1, after, 0), y_next[1]),
    ]

    def x_block(xv, half):
        at = pl.multiple_of((xv % 4) * 256, 256)
        return x_all.at[core, pl.ds(at, 256), pl.ds(half * DW, DW)]

    def x_whole(xv):
        at = pl.multiple_of((xv % 4) * 256, 256)
        return x_all.at[core, pl.ds(at, 256), :]

    near = [[], []]
    for way in range(2):
        near[way].append(send(x_block(x, 1), x_block(x, 1), x_next[way]))

    for copy in loads[4:]:
        copy.wait()
    for c in range(C):
        for i in range(6):
            keep = ku[i : i + 1, pl.ds(own_f + c * FC, FC)]
            w_u[c, i * 64 : i * 64 + 64, :] = (
                raw_u[i * 64 : i * 64 + 64, c * FC : (c + 1) * FC].astype(F32) * keep
            ).astype(BF16)
        for i in range(FC // 64):
            at = c * FC + i * 64
            keep = kd[pl.ds(own_f // 64 + at // 64, 1), :]
            w_d[at : at + 64, 0:DW] = (raw_d[at : at + 64, :].astype(F32) * keep).astype(BF16)

    for copy in far:
        copy.wait_recv()
    for way in range(2):
        near[way].append(send(x_block(x, 0), x_block(x, 0), x_next[way]))
    whole = [send(x_whole(x), x_whole(x), sibling)]
    for half in (1, 0):
        for way in range(2):
            near[way][1 - half].wait_recv()
        if half == 1:
            onward = [send(x_block(x + 1, 1), x_block(x + 1, 1), x_next[1])]
        else:
            onward.append(send(x_block(x + 3, 0), x_block(x + 3, 0), x_next[0]))
    for xv in (x + 1, x + 3):
        whole.append(send(x_whole(xv), x_whole(xv), sibling))
    for copy in onward:
        copy.wait_recv()
    whole.append(send(x_whole(x + 2), x_whole(x + 2), sibling))
    for copy in whole:
        copy.wait_recv()

    def steps_of(arr, way):
        return 4 if arr == way else 3

    def rows_of(j):
        return pl.ds(pl.multiple_of((j % Z) * TB, TB), TB)

    def pre_part(c):
        def body(i, carry):
            rows = pl.ds(pl.multiple_of(i * 256, 256), 256)
            part[c, 0, rows, :] = dot_nn(x_all[0, rows, :], w_u[c])
            part[c, 1, rows, :] = dot_nt(x_all[1, rows, :], w_d[c * FC : (c + 1) * FC, :])
            return carry

        lax.fori_loop(0, TOK // 256, body, 0)

    ring = {}

    def reduce_step(c, s):
        for arr in range(2):
            for way in range(2):
                n = steps_of(arr, way)
                if s >= n:
                    continue
                dest = z + (n - s) if way == 0 else z + Z - (n - s)
                term = part[c, arr, rows_of(dest), :]
                if s == 0:
                    src = first.at[c, arr, way]
                    src[...] = term.astype(BF16)
                else:
                    ring[c, arr, way, s - 1].wait_recv()
                    src = came.at[c, arr, way, s - 1]
                    src[...] = (src[...].astype(F32) + term).astype(BF16)
                ring[c, arr, way, s] = send(src, came.at[c, arr, way, s], z_next[way])

    def finish(c):
        total = []
        for arr in range(2):
            value = part[c, arr, rows_of(z), :]
            for way in range(2):
                last = steps_of(arr, way) - 1
                ring[c, arr, way, last].wait_recv()
                value = value + came[c, arr, way, last].astype(F32)
            total.append(value)
        activated, slope = gelu_pair(total[0])
        hid[c, 0, rows_of(z), :] = activated.astype(BF16)
        hid[c, 1, rows_of(z), :] = (total[1] * slope).astype(BF16)

    gather = {}

    def gather_step(c, s):
        for arr in range(2):
            for way in range(2):
                if s >= steps_of(arr, way):
                    continue
                if s > 0:
                    gather[c, arr, way, s - 1].wait_recv()
                source = z + Z - s if way == 0 else z + s
                block = hid.at[c, arr, rows_of(source), :]
                gather[c, arr, way, s] = send(block, block, z_next[way])

    def gather_end(c):
        for arr in range(2):
            for way in range(2):
                gather[c, arr, way, steps_of(arr, way) - 1].wait_recv()

    scale = float(TOK) ** -0.5
    grads_in = []

    def weight_grads(c):
        def up(i, carry):
            at = pl.multiple_of(i * 128, 128)
            g = dot_tn(x_all[0, :, pl.ds(at, 128)], hid[c, 1]) * scale
            gu_s[c, pl.ds(at, 128), :] = g.astype(BF16)
            return carry

        def down(i, carry):
            at = pl.multiple_of(i * 128, 128)
            g = dot_tn(hid[c, 0, :, pl.ds(at, 128)], x_all[1]) * scale
            gd_s[c, pl.ds(at, 128), :] = g.astype(BF16)
            return carry

        lax.fori_loop(0, D2 // 128, up, 0)
        lax.fori_loop(0, FC // 128, down, 0)
        grads_in.append(
            (
                send(gu_s.at[c, pl.ds(DW, DW), :], gu_r.at[c], partner),
                send(gd_s.at[c, :, pl.ds(DW, DW)], gd_r.at[c], partner),
            )
        )

    def keep_grads(c, src_u, src_d, quarter):
        mine = pl.multiple_of(quarter * FQ + c * FC, FC)
        there = pl.multiple_of((quarter % 2) * FQ + c * FC, FC)
        for i in range(6):
            keep = ku[i : i + 1, pl.ds(mine, FC)]
            gwu[i * 64 : i * 64 + 64, pl.ds(there, FC)] = (
                src_u(slice(i * 64, i * 64 + 64)).astype(F32) * keep
            ).astype(BF16)
        for i in range(FC // 64):
            keep = kd[pl.ds(mine // 64 + i, 1), :]
            gwd[pl.ds(there + i * 64, 64), :] = (
                src_d(slice(i * 64, i * 64 + 64)).astype(F32) * keep
            ).astype(BF16)

    def act_part(c):
        def body(i, carry):
            rows = pl.ds(pl.multiple_of(i * 256, 256), 256)
            o = dot_nn(hid[c, 0, rows, :], w_d[c * FC : (c + 1) * FC, :])
            g = dot_nt(hid[c, 1, rows, :], w_u[c])
            if c > 0:
                o = o + acc[0, rows, :]
                g = g + acc[1, rows, :]
            acc[0, rows, :] = o
            acc[1, rows, :] = g
            return carry

        lax.fori_loop(0, TOK // 256, body, 0)

    for c in range(C):
        for copy in weight_in[c]:
            copy.wait_recv()
        pre_part(c)
        reduce_step(c, 0)
    for s in range(1, 4):
        for c in range(C):
            reduce_step(c, s)
    for c in range(C):
        finish(c)
        gather_step(c, 0)
    for s in range(1, 4):
        for c in range(C):
            gather_step(c, s)
    for c in range(C):
        gather_end(c)
        weight_grads(c)
        act_part(c)

    def cast(i, carry):
        rows = pl.ds(pl.multiple_of(i * 256, 256), 256)
        core_s[rows, :] = acc[1 - core, rows, :].astype(BF16)
        return carry

    lax.fori_loop(0, TOK // 256, cast, 0)
    both = send(core_s, core_r, sibling)
    for c in range(C):
        keep_grads(c, lambda s: gu_s[c, s, :], lambda s: gd_s[c, s, 0:DW], y)
    both.wait_recv()

    def x_term(xv, half):
        rows = pl.ds(pl.multiple_of((xv % 4) * 256, 256), 256)
        cols = slice(half * DW, half * DW + DW)
        return acc[core, rows, cols] + core_r[rows, cols].astype(F32)

    def x_send(at, value, way):
        xs[at] = value.astype(BF16)
        return send(xs.at[at], xr.at[at], x_next[way])

    r0 = x_send(0, x_term(x + 2, 0), 0)
    l0 = x_send(1, x_term(x + 2, 1), 1)
    r1b = x_send(2, x_term(x + 1, 1), 0)
    l1a = x_send(3, x_term(x + 3, 0), 1)
    r0.wait_recv()
    r1a = x_send(4, x_term(x + 1, 0) + xr[0].astype(F32), 0)
    l0.wait_recv()
    l1b = x_send(5, x_term(x + 3, 1) + xr[1].astype(F32), 1)
    for copy in (r1b, l1a, r1a, l1b):
        copy.wait_recv()
    yfull[:, 0:DW] = x_term(x, 0) + xr[4].astype(F32) + xr[3].astype(F32)
    yfull[:, DW:D2] = x_term(x, 1) + xr[2].astype(F32) + xr[5].astype(F32)

    def y_term(half, r, p):
        at = pl.multiple_of(r * 128 + p * ROWS, ROWS)
        return yfull[pl.ds(at, ROWS), half * DW : half * DW + DW]

    def y_send(at, value, way):
        ys[at] = value.astype(BF16)
        return send(ys.at[at], yr.at[at], y_next[way])

    r0 = y_send(0, y_term(0, 0, 1 - dp), 0)
    l0 = y_send(1, y_term(0, 1, 1 - dp), 1)
    r1b = y_send(2, y_term(1, 1, p_of[0]), 0)
    l1a = y_send(3, y_term(1, 0, p_of[1]), 1)
    r0.wait_recv()
    r1a = y_send(4, y_term(1, 0, p_of[0]) + yr[0].astype(F32), 0)
    l0.wait_recv()
    l1b = y_send(5, y_term(1, 1, p_of[1]) + yr[1].astype(F32), 1)
    for copy in (r1b, l1a, r1a, l1b):
        copy.wait_recv()
    sum_0 = y_term(0, 0, dp) + yr[4].astype(F32) + yr[3].astype(F32)
    sum_1 = y_term(0, 1, dp) + yr[2].astype(F32) + yr[5].astype(F32)
    is_0 = core == 0
    fin_s[...] = jnp.where(is_0, sum_1, sum_0).astype(BF16)
    mine = jnp.where(is_0, sum_0, sum_1).astype(BF16)
    last = send(fin_s, fin_r, sibling)
    for c in range(C):
        for copy in grads_in[c]:
            copy.wait_recv()
        keep_grads(c, lambda s: gu_r[c, s, :], lambda s: gd_r[c, s, :], y + 1 - 2 * yl)
    last.wait_recv()
    theirs = fin_r[...]
    out[...] = jnp.where(is_0, mine.astype(F32), theirs.astype(F32)).astype(BF16)
    gin[...] = jnp.where(is_0, theirs.astype(F32), mine.astype(F32)).astype(BF16)

    for copy in sent:
        copy.wait_send()


def local(tokens, grad_out, w_up, w_down, mask_up, mask_down):
    keep_up = jnp.repeat(mask_up.astype(F32), BLOCK, axis=1)
    keep_down = jnp.repeat(mask_down.astype(F32), BLOCK, axis=1)
    vmem = pl.BlockSpec(memory_space=pltpu.VMEM)
    hbm = pl.BlockSpec(memory_space=pl.ANY)
    return pl.pallas_call(
        kernel,
        out_shape=(
            jax.ShapeDtypeStruct((ROWS, DW), BF16),
            jax.ShapeDtypeStruct((ROWS, DW), BF16),
            jax.ShapeDtypeStruct((DW, 2 * FQ), BF16),
            jax.ShapeDtypeStruct((2 * FQ, DW), BF16),
        ),
        in_specs=[vmem, vmem, hbm, hbm, vmem, vmem],
        out_specs=(vmem, vmem, vmem, vmem),
        scratch_shapes=[
            pltpu.VMEM((2, ROWS, DW), BF16),
            pltpu.VMEM((2, TOK, D2), BF16),
            pltpu.VMEM((DW, FQ), BF16),
            pltpu.VMEM((2, DW // 2, FQ), BF16),
            pltpu.VMEM((FQ, DW), BF16),
            pltpu.VMEM((2, FQ, DW), BF16),
            pltpu.VMEM((C, D2, FC), BF16),
            pltpu.VMEM((FQ, D2), BF16),
            pltpu.VMEM((2, C, DW // 2, FC), BF16),
            pltpu.VMEM((2, C, FC // 2, DW), BF16),
            pltpu.VMEM((C, 2, TOK, FC), F32),
            pltpu.VMEM((C, 2, 2, TB, FC), BF16),
            pltpu.VMEM((C, 2, 2, 4, TB, FC), BF16),
            pltpu.VMEM((C, 2, TOK, FC), BF16),
            pltpu.VMEM((2, TOK, D2), F32),
            pltpu.VMEM((TOK, D2), BF16),
            pltpu.VMEM((TOK, D2), BF16),
            pltpu.VMEM((6, 256, DW), BF16),
            pltpu.VMEM((6, 256, DW), BF16),
            pltpu.VMEM((256, D2), F32),
            pltpu.VMEM((6, ROWS, DW), BF16),
            pltpu.VMEM((6, ROWS, DW), BF16),
            pltpu.VMEM((ROWS, DW), BF16),
            pltpu.VMEM((ROWS, DW), BF16),
            pltpu.VMEM((C, D2, FC), BF16),
            pltpu.VMEM((C, DW, FC), BF16),
            pltpu.VMEM((C, FC, D2), BF16),
            pltpu.VMEM((C, FC, DW), BF16),
            pltpu.SemaphoreType.DMA((8,)),
            pltpu.SemaphoreType.DMA((MESSAGES,)),
            pltpu.SemaphoreType.DMA((MESSAGES,)),
        ],
        compiler_params=pltpu.CompilerParams(
            collective_id=0, has_side_effects=True, vmem_limit_bytes=56 * 1024 * 1024
        ),
        cost_estimate=pl.CostEstimate(
            flops=12 * TOK * D2 * FQ, bytes_accessed=8 * 1024 * 1024, transcendentals=TB * FQ
        ),
    )(tokens, grad_out, w_up, w_down, keep_up, keep_down)


def solution(mesh):
    in_specs = (
        P(("row", "dp"), "col"),
        P(("row", "dp"), "col"),
        P("col", "row"),
        P("row", "col"),
        P("col", "row"),
        P("row", "col"),
    )
    out_specs = (
        P(("row", "dp"), "col"),
        P(("row", "dp"), "col"),
        P("col", ("row", "dp")),
        P(("row", "dp"), "col"),
    )
    return jax.shard_map(local, mesh=mesh, in_specs=in_specs, out_specs=out_specs, check_vma=False)
```

```python
import jax
import jax.numpy as jnp
from jax import lax
from jax.experimental import pallas as pl
from jax.experimental.pallas import tpu as pltpu
from jax.sharding import PartitionSpec as P

BLOCK = 64
MESH = pl.DeviceIdType.MESH
F32 = jnp.float32
BF16 = jnp.bfloat16

COEF_ROOT = 0.7978845608028654
COEF_CUBE = 0.044715

TOK = 1024
ROWS = 64
DW = 384
D2 = 2 * DW
FQ = 768
C = 3
FC = FQ // C
Z = 8
TB = TOK // Z
MESSAGES = 200


def gelu_pair(pre_act):
    argument = COEF_ROOT * (pre_act + COEF_CUBE * pre_act * pre_act * pre_act)
    tangent = jnp.tanh(argument)
    activated = 0.5 * pre_act * (1.0 + tangent)
    gelu_slope = 0.5 * (1.0 + tangent) + 0.5 * pre_act * (1.0 - tangent * tangent) * COEF_ROOT * (
        1.0 + 3.0 * COEF_CUBE * pre_act * pre_act
    )
    return (activated, gelu_slope)


def dot_nn(a, b):
    return lax.dot_general(a, b, (((1,), (0,)), ((), ())), preferred_element_type=F32)


def dot_nt(a, b):
    return lax.dot_general(a, b, (((1,), (1,)), ((), ())), preferred_element_type=F32)


def dot_tn(a, b):
    return lax.dot_general(a, b, (((0,), (0,)), ((), ())), preferred_element_type=F32)


def repeat_masks(mask_up, mask_down, keep_up, keep_down):
    def spread(rows, cols):
        block = lax.broadcasted_iota(jnp.int32, (rows, cols), 0)
        entry = lax.broadcasted_iota(jnp.int32, (rows, cols), 1)
        return jnp.where((entry >> 6) == block, 1.0, 0.0).astype(BF16)

    keep_up[...] = dot_nn(mask_up[...].astype(F32).astype(BF16), spread(mask_up.shape[1], keep_up.shape[1]))
    keep_down[...] = dot_nn(
        mask_down[...].astype(F32).astype(BF16), spread(mask_down.shape[1], keep_down.shape[1])
    )


def kernel(
    tok, grad, wu, wd, mask_up, mask_down, acts, grads,
    ku, kd, stage, x_all, x_turned, raw_u, raw_un, raw_d, raw_dn, w_all, w_turned, w_own, w_near,
    part, first, came, swap_s, swap_r, hid, acc, xs, xr, yfull, ys, yr, fin_s, g_own, g_far,
    load_sem, send_sem, recv_sem,
):
    row, col, dp = lax.axis_index("row"), lax.axis_index("col"), lax.axis_index("dp")
    x, core = row // 2, row % 2
    yl, z = col // Z, col % Z
    y = dp * 2 + yl

    def at_y(v, k=None):
        v = v % 4
        place = {"col": (v % 2) * Z + z, "dp": v // 2}
        return place if k is None else {"row": x * 2 + k, **place}

    def at_x(v):
        return {"row": (v % 4) * 2 + core}

    def at_z(v):
        return {"col": yl * Z + v % Z}

    sibling = {"row": x * 2 + (1 - core)}
    y_next = (at_y(y + 1), at_y(y + 3))
    x_next = (at_x(x + 1), at_x(x + 3))
    z_next = (at_z(z + 1), at_z(z + Z - 1))

    count = [0]
    sent = []

    def slot(n=1):
        count[0] += n
        return count[0] - n

    def send(src, dst, device, at=None, to=None):
        at = slot() if at is None else at
        copy = pltpu.make_async_remote_copy(
            src_ref=src, dst_ref=dst, send_sem=send_sem.at[at],
            recv_sem=recv_sem.at[at if to is None else to],
            device_id=device, device_id_type=MESH,
        )
        copy.start()
        sent.append(copy)
        return copy

    def arrived(ref, at):
        pltpu.make_async_remote_copy(
            src_ref=ref, dst_ref=ref, send_sem=send_sem.at[at], recv_sem=recv_sem.at[at],
            device_id=sibling, device_id_type=MESH,
        ).wait_recv()

    own_f = pl.multiple_of(y * FQ, FQ)
    near_f = [pl.multiple_of(((y + 1) % 4) * FQ, FQ), pl.multiple_of(((y + 3) % 4) * FQ, FQ)]
    loads = []

    def load(src, dst):
        copy = pltpu.make_async_copy(src, dst, load_sem.at[len(loads)])
        copy.start()
        loads.append(copy)

    for way in range(2):
        load(wu.at[:, pl.ds(near_f[way], FQ)], raw_un.at[way])
        load(wd.at[pl.ds(near_f[way], FQ), :], raw_dn.at[way])
    load(wu.at[:, pl.ds(own_f, FQ)], raw_u)
    load(wd.at[pl.ds(own_f, FQ), :], raw_d)

    barrier = pltpu.get_barrier_semaphore()
    greeted = (sibling, *x_next, *z_next, *(at_y(y + d, k) for d in (1, 3) for k in (0, 1)))
    for other in greeted:
        pl.semaphore_signal(barrier, inc=1, device_id=other, device_id_type=MESH)

    def block(xv, r, p, half):
        at = pl.multiple_of(p * 512 + (xv % 4) * 128 + r * ROWS, ROWS)
        return x_all.at[pl.ds(at, ROWS), pl.ds(half * DW, DW)]

    def unit(xv, p, half):
        at = pl.multiple_of(p * 512 + (xv % 4) * 128, 128)
        return x_all.at[pl.ds(at, 128), pl.ds(half * DW, DW)]

    stage[0] = tok[...]
    stage[1] = grad[...]
    own_rows = pl.multiple_of(dp * 512 + row * ROWS, ROWS)
    x_all[pl.ds(own_rows, ROWS), 0:DW] = stage[core]
    pl.semaphore_wait(barrier, len(greeted))

    swap = send(stage.at[1 - core], block(x, core, dp, 0), sibling)
    step = [send(block(x, core, dp, 0), block(x, core, dp, 1), y_next[way]) for way in range(2)]
    repeat_masks(mask_up, mask_down, ku, kd)
    swap.wait_recv()
    for way in range(2):
        step.append(send(block(x, 1 - core, dp, 0), block(x, 1 - core, dp, 1), y_next[way]))

    near = {}

    def near_send(p, half, name):
        near[name] = [send(unit(x, p, half), unit(x, p, half), x_next[way]) for way in range(2)]

    near_send(dp, 0, "own")

    near_slots = {}

    def near_weights(c):
        for way in range(2):
            f_at = c * FC + way * 128
            for i in range(6):
                keep = ku[i : i + 1, pl.ds(near_f[way] + f_at, 128)]
                w_near[c, way, 0, i * 64 : i * 64 + 64, :] = (
                    raw_un[way, i * 64 : i * 64 + 64, f_at : f_at + 128].astype(F32) * keep
                ).astype(BF16)
            rows = []
            for i in range(2):
                keep = kd[pl.ds(near_f[way] // 64 + f_at // 64 + i, 1), :]
                rows.append(raw_dn[way, f_at + i * 64 : f_at + i * 64 + 64, :].astype(F32) * keep)
            w_near[c, way, 1] = jnp.concatenate(rows, 0).T.astype(BF16)

    def send_weights(c):
        for way in range(2):
            base = slot(2)
            near_slots[c, way] = base
            for arr in range(2):
                send(
                    w_near.at[c, way, arr],
                    w_all.at[c, core, pl.ds(DW, DW), pl.ds(way * 128, 128)],
                    at_y(y + (1 if way == 0 else 3), arr),
                    base + arr,
                    base + core,
                )

    own_in = {}

    def own_weights(c):
        for i in range(6):
            keep = ku[i : i + 1, pl.ds(own_f + c * FC, FC)]
            w_own[c, 0, i * 64 : i * 64 + 64, :] = (
                raw_u[i * 64 : i * 64 + 64, c * FC : (c + 1) * FC].astype(F32) * keep
            ).astype(BF16)
        rows = []
        for i in range(FC // 64):
            at = c * FC + i * 64
            keep = kd[pl.ds(own_f // 64 + at // 64, 1), :]
            rows.append(raw_d[at : at + 64, :].astype(F32) * keep)
        w_own[c, 1] = jnp.concatenate(rows, 0).T.astype(BF16)
        own_in[c] = send(w_own.at[c, 1 - core], w_all.at[c, core, pl.ds(0, DW), :], sibling)
        w_all[c, core, 0:DW, :] = w_own[c, core]

    def weights_in(c):
        own_in[c].wait_recv()
        for way in range(2):
            for r in range(2):
                arrived(
                    w_all.at[c, r, pl.ds(DW, DW), pl.ds(way * 128, 128)], near_slots[c, way] + r
                )

    for copy in loads[:4]:
        copy.wait()
    near_weights(0)
    for copy in step:
        copy.wait_recv()
    before, after = ((y + 3) % 4) // 2, ((y + 1) % 4) // 2
    far = [
        send(block(x, 0, before, 1), block(x, 0, before, 0), y_next[0]),
        send(block(x, 1, after, 1), block(x, 1, after, 0), y_next[1]),
    ]
    near_send(0, 1, "zero")
    near_send(1, 1, "one")
    send_weights(0)
    for copy in loads[4:]:
        copy.wait()
    own_weights(0)
    for copy in far:
        copy.wait_recv()
    near_send(1 - dp, 0, "far")
    near_weights(1)
    send_weights(1)
    onward = []

    def pass_on(name, p, half, way):
        for copy in near[name]:
            copy.wait_recv()
        there = x + 3 if way == 0 else x + 1
        onward.append(send(unit(there, p, half), unit(there, p, half), x_next[way]))

    pass_on("own", dp, 0, 0)
    pass_on("zero", 0, 1, 1)
    own_weights(1)
    pass_on("one", 1, 1, 0)
    near_weights(2)
    send_weights(2)
    pass_on("far", 1 - dp, 0, 1)
    own_weights(2)
    for copy in onward:
        copy.wait_recv()

    def steps_of(r, way):
        return 4 if r == way else 3

    def rows_of(j):
        return pl.ds(pl.multiple_of((j % Z) * TB, TB), TB)

    def pre_part(c):
        weights_in(c)

        def body(i, carry):
            rows = pl.ds(pl.multiple_of(i * 256, 256), 256)
            for r in range(2):
                part[c, r, rows, :] = dot_nn(x_all[rows, :], w_all[c, r])
            return carry

        lax.fori_loop(0, TOK // 256, body, 0)

    ring = {}

    def reduce_step(c, s):
        for r in range(2):
            for way in range(2):
                n = steps_of(r, way)
                if s >= n:
                    continue
                dest = z + (n - s) if way == 0 else z + Z - (n - s)
                term = part[c, r, rows_of(dest), :]
                if s == 0:
                    src = first.at[c, r, way]
                    src[...] = term.astype(BF16)
                else:
                    ring[c, r, way, s - 1].wait_recv()
                    src = came.at[c, r, way, s - 1]
                    src[...] = (src[...].astype(F32) + term).astype(BF16)
                ring[c, r, way, s] = send(src, came.at[c, r, way, s], z_next[way])

    swaps = {}

    def finish(c):
        for r in range(2):
            value = part[c, r, rows_of(z), :]
            for way in range(2):
                last = steps_of(r, way) - 1
                ring[c, r, way, last].wait_recv()
                value = value + came[c, r, way, last].astype(F32)
            swap_s[c, r] = value
        swaps[c] = send(swap_s.at[c], swap_r.at[c], sibling)

    gather = {}

    def activate(c):
        swaps[c].wait_recv()
        for r in range(2):
            mine, theirs = swap_s[c, r], swap_r[c, r]
            pre_act = jnp.where(core == 0, mine, theirs)
            grad_hidden = jnp.where(core == 0, theirs, mine)
            activated, slope = gelu_pair(pre_act)
            value = jnp.where(core == 0, grad_hidden * slope, activated)
            hid[c, r, rows_of(z), :] = value.astype(BF16)

    def gather_step(c, s):
        for r in range(2):
            for way in range(2):
                if s >= steps_of(r, way):
                    continue
                if s > 0:
                    gather[c, r, way, s - 1].wait_recv()
                source = z + Z - s if way == 0 else z + s
                part_of = hid.at[c, r, rows_of(source), :]
                gather[c, r, way, s] = send(part_of, part_of, z_next[way])

    def gather_end(c):
        for r in range(2):
            for way in range(2):
                gather[c, r, way, steps_of(r, way) - 1].wait_recv()

    def turn_tokens():
        for i in range(8):
            x_turned[:, i * 128 : i * 128 + 128] = x_all[i * 128 : i * 128 + 128, :].T

    def turn_weights(c):
        for r in range(2):
            w_turned[c, r] = w_all[c, r].T

    scale = float(TOK) ** -0.5
    grads_in = []

    def weight_grads(c):
        def width(dst, first_row):
            def body(i, carry):
                rows = pl.ds(pl.multiple_of(i * 128, 128), 128)
                wide = pl.ds(pl.multiple_of(first_row + i * 128, 128), 128)
                for r in range(2):
                    g = dot_nn(x_turned[wide, :], hid[c, r]) * scale
                    dst[c, r, rows, :] = g.astype(BF16)
                return carry

            lax.fori_loop(0, DW // 128, body, 0)

        width(g_far, DW)
        base = slot(2)
        for r in range(2):
            send(g_far.at[c, r], grads.at[core, 1, c], at_y(y + 1 - 2 * yl, r), base + r, base + core)
        width(g_own, 0)
        across = send(g_own.at[c, 1 - core], grads.at[core, 0, c], sibling)
        grads[core, 0, c] = g_own[c, core]
        grads_in.append((base, across))

    def grads_arrived(c):
        base, across = grads_in[c]
        across.wait_recv()
        for arr in range(2):
            arrived(grads.at[arr, 1, c], base + arr)

    def act_part(c):
        def body(i, carry):
            rows = pl.ds(pl.multiple_of(i * 256, 256), 256)
            o = dot_nn(hid[c, 0, rows, :], w_turned[c, 0]) + dot_nn(hid[c, 1, rows, :], w_turned[c, 1])
            acc[rows, :] = o if c == 0 else o + acc[rows, :]
            return carry

        lax.fori_loop(0, TOK // 256, body, 0)

    pre_part(0)
    reduce_step(0, 0)
    pre_part(1)
    reduce_step(1, 0)
    reduce_step(0, 1)
    pre_part(2)
    reduce_step(2, 0)
    reduce_step(1, 1)
    turn_tokens()
    reduce_step(0, 2)
    reduce_step(2, 1)
    turn_weights(0)
    reduce_step(1, 2)
    reduce_step(0, 3)
    turn_weights(1)
    reduce_step(2, 2)
    reduce_step(1, 3)
    finish(0)
    turn_weights(2)
    reduce_step(2, 3)
    finish(1)
    activate(0)
    gather_step(0, 0)
    finish(2)
    activate(1)
    gather_step(1, 0)
    gather_step(0, 1)
    activate(2)
    gather_step(2, 0)
    gather_step(0, 2)
    gather_step(1, 1)
    gather_step(0, 3)
    gather_step(2, 1)
    gather_step(1, 2)
    gather_end(0)
    weight_grads(0)
    gather_step(2, 2)
    gather_step(1, 3)
    act_part(0)
    gather_step(2, 3)
    gather_end(1)
    weight_grads(1)
    act_part(1)
    gather_end(2)
    act_part(2)

    def x_term(xv, p):
        return acc[pl.ds(pl.multiple_of(p * 512 + (xv % 4) * 128, 128), 128), :]

    def x_send(at, value, way):
        xs[at] = value.astype(BF16)
        return send(xs.at[at], xr.at[at], x_next[way])

    r0 = x_send(0, x_term(x + 2, 0), 0)
    l0 = x_send(1, x_term(x + 2, 1), 1)
    r1b = x_send(2, x_term(x + 1, 1), 0)
    l1a = x_send(3, x_term(x + 3, 0), 1)
    weight_grads(2)
    r0.wait_recv()
    r1a = x_send(4, x_term(x + 1, 0) + xr[0].astype(F32), 0)
    l0.wait_recv()
    l1b = x_send(5, x_term(x + 3, 1) + xr[1].astype(F32), 1)
    for copy in (r1b, l1a, r1a, l1b):
        copy.wait_recv()
    yfull[0:128, :] = x_term(x, 0) + xr[4].astype(F32) + xr[3].astype(F32)
    yfull[128:256, :] = x_term(x, 1) + xr[2].astype(F32) + xr[5].astype(F32)

    def y_term(half, r, p):
        at = pl.multiple_of(p * 128 + r * ROWS, ROWS)
        return yfull[pl.ds(at, ROWS), half * DW : half * DW + DW]

    def y_send(at, value, way):
        ys[at] = value.astype(BF16)
        return send(ys.at[at], yr.at[at], y_next[way])

    r0 = y_send(0, y_term(0, 0, 1 - dp), 0)
    l0 = y_send(1, y_term(0, 1, 1 - dp), 1)
    r1b = y_send(2, y_term(1, 1, after), 0)
    l1a = y_send(3, y_term(1, 0, before), 1)
    r0.wait_recv()
    r1a = y_send(4, y_term(1, 0, after) + yr[0].astype(F32), 0)
    l0.wait_recv()
    l1b = y_send(5, y_term(1, 1, before) + yr[1].astype(F32), 1)
    for copy in (r1b, l1a, r1a, l1b):
        copy.wait_recv()
    sum_0 = y_term(0, 0, dp) + yr[4].astype(F32) + yr[3].astype(F32)
    sum_1 = y_term(0, 1, dp) + yr[2].astype(F32) + yr[5].astype(F32)
    fin_s[...] = jnp.where(core == 0, sum_1, sum_0).astype(BF16)
    acts[core] = jnp.where(core == 0, sum_0, sum_1).astype(BF16)
    last = send(fin_s, acts.at[core], sibling)
    for c in range(C):
        grads_arrived(c)
    last.wait_recv()

    for copy in sent:
        copy.wait_send()


def place_kernel(acts, grads, mask_up, mask_down, out, gin, gwu, gwd, ku, kd):
    row, col, dp = lax.axis_index("row"), lax.axis_index("col"), lax.axis_index("dp")
    yl = col // Z
    repeat_masks(mask_up, mask_down, ku, kd)
    gin[...] = acts[0]
    out[...] = acts[1]
    for quarter in range(2):
        which = yl if quarter == 0 else 1 - yl
        for c in range(C):
            there = pl.multiple_of(which * FQ + c * FC, FC)
            mine = pl.multiple_of(dp * 2 * FQ + which * FQ + c * FC, FC)
            for i in range(6):
                keep = ku[i : i + 1, pl.ds(mine, FC)]
                rows = slice(i * 64, i * 64 + 64)
                gwu[rows, pl.ds(there, FC)] = (
                    grads[0, quarter, c, rows, :].astype(F32) * keep
                ).astype(BF16)
            turned = grads[1, quarter, c].astype(F32).T
            for i in range(FC // 64):
                keep = kd[pl.ds(mine // 64 + i, 1), :]
                gwd[pl.ds(there + i * 64, 64), :] = (
                    turned[i * 64 : i * 64 + 64, :] * keep
                ).astype(BF16)


def local(tokens, grad_out, w_up, w_down, mask_up, mask_down):
    vmem = pl.BlockSpec(memory_space=pltpu.VMEM)
    hbm = pl.BlockSpec(memory_space=pl.ANY)
    keeps = [pltpu.VMEM((6, 4 * FQ), F32), pltpu.VMEM((48, DW), F32)]
    acts, grads = pl.pallas_call(
        kernel,
        out_shape=(
            jax.ShapeDtypeStruct((2, ROWS, DW), BF16),
            jax.ShapeDtypeStruct((2, 2, C, DW, FC), BF16),
        ),
        in_specs=[vmem, vmem, hbm, hbm, vmem, vmem],
        out_specs=(vmem, vmem),
        scratch_shapes=[
            *keeps,
            pltpu.VMEM((2, ROWS, DW), BF16),
            pltpu.VMEM((TOK, D2), BF16),
            pltpu.VMEM((D2, TOK), BF16),
            pltpu.VMEM((DW, FQ), BF16),
            pltpu.VMEM((2, DW, FQ), BF16),
            pltpu.VMEM((FQ, DW), BF16),
            pltpu.VMEM((2, FQ, DW), BF16),
            pltpu.VMEM((C, 2, D2, FC), BF16),
            pltpu.VMEM((C, 2, FC, D2), BF16),
            pltpu.VMEM((C, 2, DW, FC), BF16),
            pltpu.VMEM((C, 2, 2, DW, 128), BF16),
            pltpu.VMEM((C, 2, TOK, FC), F32),
            pltpu.VMEM((C, 2, 2, TB, FC), BF16),
            pltpu.VMEM((C, 2, 2, 4, TB, FC), BF16),
            pltpu.VMEM((C, 2, TB, FC), F32),
            pltpu.VMEM((C, 2, TB, FC), F32),
            pltpu.VMEM((C, 2, TOK, FC), BF16),
            pltpu.VMEM((TOK, D2), F32),
            pltpu.VMEM((6, 128, D2), BF16),
            pltpu.VMEM((6, 128, D2), BF16),
            pltpu.VMEM((256, D2), F32),
            pltpu.VMEM((6, ROWS, DW), BF16),
            pltpu.VMEM((6, ROWS, DW), BF16),
            pltpu.VMEM((ROWS, DW), BF16),
            pltpu.VMEM((C, 2, DW, FC), BF16),
            pltpu.VMEM((C, 2, DW, FC), BF16),
            pltpu.SemaphoreType.DMA((8,)),
            pltpu.SemaphoreType.DMA((MESSAGES,)),
            pltpu.SemaphoreType.DMA((MESSAGES,)),
        ],
        compiler_params=pltpu.CompilerParams(
            collective_id=0, has_side_effects=True, vmem_limit_bytes=56 * 1024 * 1024
        ),
        cost_estimate=pl.CostEstimate(
            flops=12 * TOK * D2 * FQ, bytes_accessed=8 * 1024 * 1024, transcendentals=TB * FQ
        ),
    )(tokens, grad_out, w_up, w_down, mask_up, mask_down)
    return pl.pallas_call(
        place_kernel,
        out_shape=(
            jax.ShapeDtypeStruct((ROWS, DW), BF16),
            jax.ShapeDtypeStruct((ROWS, DW), BF16),
            jax.ShapeDtypeStruct((DW, 2 * FQ), BF16),
            jax.ShapeDtypeStruct((2 * FQ, DW), BF16),
        ),
        in_specs=[vmem] * 4,
        out_specs=(vmem,) * 4,
        scratch_shapes=keeps,
        compiler_params=pltpu.CompilerParams(vmem_limit_bytes=32 * 1024 * 1024),
    )(acts, grads, mask_up, mask_down)


def solution(mesh):
    in_specs = (
        P(("row", "dp"), "col"),
        P(("row", "dp"), "col"),
        P("col", "row"),
        P("row", "col"),
        P("col", "row"),
        P("row", "col"),
    )
    out_specs = (
        P(("row", "dp"), "col"),
        P(("row", "dp"), "col"),
        P("col", ("row", "dp")),
        P(("row", "dp"), "col"),
    )
    return jax.shard_map(local, mesh=mesh, in_specs=in_specs, out_specs=out_specs, check_vma=False)
```

```python
import jax
import jax.numpy as jnp
from jax import lax
from jax.experimental import pallas as pl
from jax.experimental.pallas import tpu as pltpu
from jax.sharding import PartitionSpec as P

BLOCK = 64
MESH = pl.DeviceIdType.MESH
F32 = jnp.float32
BF16 = jnp.bfloat16

COEF_ROOT = 0.7978845608028654
COEF_CUBE = 0.044715

TOK = 1024
ROWS = 64
DW = 384
D2 = 2 * DW
FQ = 768
C = 3
FC = FQ // C
Z = 8
TB = TOK // Z
MESSAGES = 155
SENDS = 40


def gelu_pair(pre_act):
    argument = COEF_ROOT * (pre_act + COEF_CUBE * pre_act * pre_act * pre_act)
    tangent = jnp.tanh(argument)
    activated = 0.5 * pre_act * (1.0 + tangent)
    gelu_slope = 0.5 * (1.0 + tangent) + 0.5 * pre_act * (1.0 - tangent * tangent) * COEF_ROOT * (
        1.0 + 3.0 * COEF_CUBE * pre_act * pre_act
    )
    return (activated, gelu_slope)


def dot_nn(a, b):
    return lax.dot_general(a, b, (((1,), (0,)), ((), ())), preferred_element_type=F32)


def dot_nt(a, b):
    return lax.dot_general(a, b, (((1,), (1,)), ((), ())), preferred_element_type=F32)


def dot_tn(a, b):
    return lax.dot_general(a, b, (((0,), (0,)), ((), ())), preferred_element_type=F32)


def repeat_masks(mask_up, mask_down, keep_up, keep_down):
    def spread(rows, cols):
        block = lax.broadcasted_iota(jnp.int32, (rows, cols), 0)
        entry = lax.broadcasted_iota(jnp.int32, (rows, cols), 1)
        return jnp.where((entry >> 6) == block, 1.0, 0.0).astype(BF16)

    keep_up[...] = dot_nn(mask_up[...].astype(F32).astype(BF16), spread(mask_up.shape[1], keep_up.shape[1]))
    keep_down[...] = dot_tn(
        mask_down[...].astype(F32).astype(BF16), spread(mask_down.shape[0], keep_down.shape[1])
    )


def kernel(
    tok, grad, wu, wd, mask_up, mask_down, acts, grads,
    ku, kd, stage, x_all, x_turned, raw_u, raw_un, raw_d, raw_dn, w_all, w_turned, w_own, w_near,
    part, first, came, swap_s, swap_r, hid, acc, xs, xr, yfull, ys, yr, g_own, g_far,
    load_sem, send_sem, recv_sem,
):
    row, col, dp = lax.axis_index("row"), lax.axis_index("col"), lax.axis_index("dp")
    x, core = row // 2, row % 2
    yl, z = col // Z, col % Z
    y = dp * 2 + yl

    def at_y(v, k=None):
        v = v % 4
        place = {"col": (v % 2) * Z + z, "dp": v // 2}
        return place if k is None else {"row": x * 2 + k, **place}

    def at_x(v, k=None):
        return {"row": (v % 4) * 2 + (core if k is None else k)}

    def at_z(v):
        return {"col": yl * Z + v % Z}

    sibling = {"row": x * 2 + (1 - core)}
    y_next = (at_y(y + 1), at_y(y + 3))
    x_next = (at_x(x + 1), at_x(x + 3))
    z_next = (at_z(z + 1), at_z(z + Z - 1))

    count = [0, 0]
    sent = [None] * SENDS

    def slot(n=1):
        count[0] += n
        return count[0] - n

    def send(src, dst, device, to=None):
        at = count[1] % SENDS
        count[1] += 1
        if sent[at] is not None:
            sent[at].wait_send()
        copy = pltpu.make_async_remote_copy(
            src_ref=src, dst_ref=dst, send_sem=send_sem.at[at],
            recv_sem=recv_sem.at[slot() if to is None else to],
            device_id=device, device_id_type=MESH,
        )
        copy.start()
        sent[at] = copy
        return copy

    def arrived(ref, at):
        pltpu.make_async_remote_copy(
            src_ref=ref, dst_ref=ref, send_sem=send_sem.at[0], recv_sem=recv_sem.at[at],
            device_id=sibling, device_id_type=MESH,
        ).wait_recv()

    own_f = pl.multiple_of(y * FQ, FQ)
    near_f = [pl.multiple_of(((y + 1) % 4) * FQ, FQ), pl.multiple_of(((y + 3) % 4) * FQ, FQ)]
    loads = []

    def load(src, dst):
        copy = pltpu.make_async_copy(src, dst, load_sem.at[len(loads)])
        copy.start()
        loads.append(copy)

    for way in range(2):
        load(wu.at[:, pl.ds(near_f[way], FQ)], raw_un.at[way])
        load(wd.at[pl.ds(near_f[way], FQ), :], raw_dn.at[way])
    load(wu.at[:, pl.ds(own_f, FQ)], raw_u)
    load(wd.at[pl.ds(own_f, FQ), :], raw_d)

    barrier = pltpu.get_barrier_semaphore()
    greeted = [sibling, *z_next]
    greeted += [at_y(y + d, k) for d in (1, 2, 3) for k in (0, 1)]
    greeted += [at_x(x + d, k) for d in (1, 2, 3) for k in (0, 1)]
    for other in greeted:
        pl.semaphore_signal(barrier, inc=1, device_id=other, device_id_type=MESH)

    def block(xv, r, p, half):
        at = pl.multiple_of(p * 512 + (xv % 4) * 128 + r * ROWS, ROWS)
        return x_all.at[pl.ds(at, ROWS), pl.ds(pl.multiple_of(half * DW, DW), DW)]

    stage[0] = tok[...]
    stage[1] = grad[...]
    own_rows = pl.multiple_of(dp * 512 + row * ROWS, ROWS)
    x_all[pl.ds(own_rows, ROWS), 0:DW] = stage[core]
    pl.semaphore_wait(barrier, len(greeted))

    swap = send(stage.at[1 - core], block(x, core, dp, 0), sibling)
    first_trip = {}
    for d in (1, 3, 2):
        base = slot(2)
        first_trip[d] = base
        to_x, to_y = (x + core * d) % 4, (y + (1 - core) * d) % 4
        for arr in range(2):
            send(
                stage.at[arr],
                block(x, core, dp, (1 - core) * (d % 2)),
                {"row": to_x * 2 + arr, "col": (to_y % 2) * Z + z, "dp": to_y // 2},
                base + core,
            )
    repeat_masks(mask_up, mask_down, ku, kd)

    def trip_in(d):
        for r in range(2):
            arrived(block(x, r, dp, 0), first_trip[d] + r)

    before, after = ((y + 3) % 4) // 2, ((y + 1) % 4) // 2
    near_x, near_y, onward = {}, {}, []

    def send_x(name, p, half):
        near_x[name] = [
            send(block(x, 0, p, half), block(x, 0, p, half), x_next[way]) for way in range(2)
        ]

    def send_y(d):
        near_y[d] = [
            send(block(x + d, 1, dp, 0), block(x + d, 1, dp, 1), y_next[way]) for way in range(2)
        ]

    def on_x(name, p, half, way):
        for copy in near_x[name]:
            copy.wait_recv()
        there = x + 3 if way == 0 else x + 1
        onward.append(send(block(there, 0, p, half), block(there, 0, p, half), x_next[way]))

    def on_y(d, way):
        for copy in near_y[d]:
            copy.wait_recv()
        p = before if way == 0 else after
        onward.append(send(block(x + d, 1, p, 1), block(x + d, 1, p, 0), y_next[way]))

    near_slots = {}

    def near_weights(c):
        for way in range(2):
            f_at = c * FC + way * 128
            for i in range(6):
                keep = ku[i : i + 1, pl.ds(near_f[way] + f_at, 128)]
                w_near[c, way, 0, i * 64 : i * 64 + 64, :] = (
                    raw_un[way, i * 64 : i * 64 + 64, f_at : f_at + 128].astype(F32) * keep
                ).astype(BF16)
            rows = []
            for i in range(2):
                keep = kd[pl.ds(near_f[way] // 64 + f_at // 64 + i, 1), :]
                rows.append(raw_dn[way, f_at + i * 64 : f_at + i * 64 + 64, :].astype(F32) * keep)
            w_near[c, way, 1] = jnp.concatenate(rows, 0).T.astype(BF16)

    def send_weights(c):
        for way in range(2):
            base = slot(2)
            near_slots[c, way] = base
            for arr in range(2):
                send(
                    w_near.at[c, way, arr],
                    w_all.at[c, core, pl.ds(DW, DW), pl.ds(way * 128, 128)],
                    at_y(y + (1 if way == 0 else 3), arr),
                    base + core,
                )

    own_in = {}

    def own_weights(c):
        for i in range(6):
            keep = ku[i : i + 1, pl.ds(own_f + c * FC, FC)]
            w_own[c, 0, i * 64 : i * 64 + 64, :] = (
                raw_u[i * 64 : i * 64 + 64, c * FC : (c + 1) * FC].astype(F32) * keep
            ).astype(BF16)
        rows = []
        for i in range(FC // 64):
            at = c * FC + i * 64
            keep = kd[pl.ds(own_f // 64 + at // 64, 1), :]
            rows.append(raw_d[at : at + 64, :].astype(F32) * keep)
        w_own[c, 1] = jnp.concatenate(rows, 0).T.astype(BF16)
        own_in[c] = send(w_own.at[c, 1 - core], w_all.at[c, core, pl.ds(0, DW), :], sibling)
        w_all[c, core, 0:DW, :] = w_own[c, core]

    def weights_in(c):
        own_in[c].wait_recv()
        for way in range(2):
            for r in range(2):
                arrived(
                    w_all.at[c, r, pl.ds(DW, DW), pl.ds(way * 128, 128)], near_slots[c, way] + r
                )

    swap.wait_recv()
    send_x("own", dp, 0)
    send_y(0)
    for copy in loads[:4]:
        copy.wait()
    near_weights(0)
    send_weights(0)
    trip_in(1)
    trip_in(3)
    send_x("after", after, 1)
    send_x("before", before, 1)
    send_y(1)
    send_y(3)
    trip_in(2)
    send_x("far", 1 - dp, 0)
    send_y(2)
    on_x("own", dp, 0, 0)
    on_y(0, 0)
    for copy in loads[4:]:
        copy.wait()
    own_weights(0)
    near_weights(1)
    on_x("after", after, 1, 0)
    on_y(1, 0)
    on_x("before", before, 1, 1)
    on_y(3, 1)
    on_x("far", 1 - dp, 0, 1)
    on_y(2, 1)
    send_weights(1)
    own_weights(1)
    near_weights(2)
    send_weights(2)
    own_weights(2)
    for copy in onward:
        copy.wait_recv()

    def steps_of(r, way):
        return 4 if r == way else 3

    def rows_of(j):
        return pl.ds(pl.multiple_of((j % Z) * TB, TB), TB)

    def pre_part(c):
        weights_in(c)

        def body(i, carry):
            rows = pl.ds(pl.multiple_of(i * 256, 256), 256)
            for r in range(2):
                part[c, r, rows, :] = dot_nn(x_all[rows, :], w_all[c, r])
            return carry

        lax.fori_loop(0, TOK // 256, body, 0)

    ring = {}

    def reduce_step(c, s):
        for r in range(2):
            for way in range(2):
                n = steps_of(r, way)
                if s >= n:
                    continue
                dest = z + (n - s) if way == 0 else z + Z - (n - s)
                term = part[c, r, rows_of(dest), :]
                if s == 0:
                    src = first.at[c, r, way]
                    src[...] = term.astype(BF16)
                else:
                    ring[c, r, way, s - 1].wait_recv()
                    src = came.at[c, r, way, s - 1]
                    src[...] = (src[...].astype(F32) + term).astype(BF16)
                ring[c, r, way, s] = send(src, came.at[c, r, way, s], z_next[way])

    swaps = {}

    def finish(c):
        for r in range(2):
            value = part[c, r, rows_of(z), :]
            for way in range(2):
                last = steps_of(r, way) - 1
                ring[c, r, way, last].wait_recv()
                value = value + came[c, r, way, last].astype(F32)
            swap_s[c, r] = value
        swaps[c] = send(swap_s.at[c], swap_r.at[c], sibling)

    gather = {}

    def activate(c):
        swaps[c].wait_recv()
        for r in range(2):
            mine, theirs = swap_s[c, r], swap_r[c, r]
            pre_act = jnp.where(core == 0, mine, theirs)
            grad_hidden = jnp.where(core == 0, theirs, mine)
            activated, slope = gelu_pair(pre_act)
            value = jnp.where(core == 0, grad_hidden * slope, activated)
            hid[c, r, rows_of(z), :] = value.astype(BF16)

    def gather_step(c, s):
        for r in range(2):
            for way in range(2):
                if s >= steps_of(r, way):
                    continue
                if s > 0:
                    gather[c, r, way, s - 1].wait_recv()
                source = z + Z - s if way == 0 else z + s
                part_of = hid.at[c, r, rows_of(source), :]
                gather[c, r, way, s] = send(part_of, part_of, z_next[way])

    def gather_end(c):
        for r in range(2):
            for way in range(2):
                gather[c, r, way, steps_of(r, way) - 1].wait_recv()

    def turn_tokens():
        for i in range(8):
            x_turned[:, i * 128 : i * 128 + 128] = x_all[i * 128 : i * 128 + 128, :].T

    def turn_weights(c):
        for r in range(2):
            w_turned[c, r] = w_all[c, r].T

    scale = float(TOK) ** -0.5
    grads_in = []

    def weight_grads(c):
        def width(dst, first_row):
            def body(i, carry):
                rows = pl.ds(pl.multiple_of(i * 128, 128), 128)
                wide = pl.ds(pl.multiple_of(first_row + i * 128, 128), 128)
                for r in range(2):
                    g = dot_nn(x_turned[wide, :], hid[c, r]) * scale
                    dst[c, r, rows, :] = g.astype(BF16)
                return carry

            lax.fori_loop(0, DW // 128, body, 0)

        width(g_far, DW)
        base = slot(2)
        for r in range(2):
            send(g_far.at[c, r], grads.at[core, 1, c], at_y(y + 1 - 2 * yl, r), base + core)
        width(g_own, 0)
        across = send(g_own.at[c, 1 - core], grads.at[core, 0, c], sibling)
        grads[core, 0, c] = g_own[c, core]
        grads_in.append((base, across))

    def grads_arrived(c):
        base, across = grads_in[c]
        across.wait_recv()
        for arr in range(2):
            arrived(grads.at[arr, 1, c], base + arr)

    def act_part(c):
        def body(i, carry):
            rows = pl.ds(pl.multiple_of(i * 256, 256), 256)
            o = dot_nn(hid[c, 0, rows, :], w_turned[c, 0]) + dot_nn(hid[c, 1, rows, :], w_turned[c, 1])
            acc[rows, :] = o if c == 0 else o + acc[rows, :]
            return carry

        lax.fori_loop(0, TOK // 256, body, 0)

    pre_part(0)
    reduce_step(0, 0)
    pre_part(1)
    reduce_step(1, 0)
    reduce_step(0, 1)
    pre_part(2)
    reduce_step(2, 0)
    reduce_step(1, 1)
    turn_tokens()
    reduce_step(0, 2)
    reduce_step(2, 1)
    turn_weights(0)
    reduce_step(1, 2)
    reduce_step(0, 3)
    turn_weights(1)
    reduce_step(2, 2)
    reduce_step(1, 3)
    finish(0)
    turn_weights(2)
    reduce_step(2, 3)
    finish(1)
    activate(0)
    gather_step(0, 0)
    finish(2)
    activate(1)
    gather_step(1, 0)
    gather_step(0, 1)
    activate(2)
    gather_step(2, 0)
    gather_step(0, 2)
    gather_step(1, 1)
    gather_step(0, 3)
    gather_step(2, 1)
    gather_step(1, 2)
    gather_end(0)
    weight_grads(0)
    gather_step(2, 2)
    gather_step(1, 3)
    act_part(0)
    gather_step(2, 3)
    gather_end(1)
    weight_grads(1)
    act_part(1)
    gather_end(2)
    act_part(2)

    def x_term(xv, p):
        return acc[pl.ds(pl.multiple_of(p * 512 + (xv % 4) * 128, 128), 128), :]

    def x_send(at, value, way):
        xs[at] = value.astype(BF16)
        return send(xs.at[at], xr.at[at], x_next[way])

    r0 = x_send(0, x_term(x + 2, 0), 0)
    l0 = x_send(1, x_term(x + 2, 1), 1)
    r1b = x_send(2, x_term(x + 1, 1), 0)
    l1a = x_send(3, x_term(x + 3, 0), 1)
    weight_grads(2)
    r0.wait_recv()
    r1a = x_send(4, x_term(x + 1, 0) + xr[0].astype(F32), 0)
    l0.wait_recv()
    l1b = x_send(5, x_term(x + 3, 1) + xr[1].astype(F32), 1)
    for copy in (r1b, l1a, r1a, l1b):
        copy.wait_recv()
    yfull[0:128, :] = x_term(x, 0) + xr[4].astype(F32) + xr[3].astype(F32)
    yfull[128:256, :] = x_term(x, 1) + xr[2].astype(F32) + xr[5].astype(F32)

    def y_term(half, r, p):
        at = pl.multiple_of(p * 128 + r * ROWS, ROWS)
        return yfull[pl.ds(at, ROWS), half * DW : half * DW + DW].astype(BF16)

    last = []
    for d, half, p in ((2, 0, 1 - dp), (1, 1, after), (3, 1, before)):
        base = slot(2)
        last.append((d, base))
        for r in range(2):
            ys[d, r] = y_term(half, r, p)
            send(ys.at[d, r], yr.at[core, d], at_y(y + d, r), base + core)
    ys[0, 0] = y_term(0, 1 - core, dp)
    across = send(ys.at[0, 0], yr.at[core, 0], sibling)
    yr[core, 0] = y_term(0, core, dp)
    for d, base in last:
        for arr in range(2):
            arrived(yr.at[arr, d], base + arr)
    across.wait_recv()
    for arr in range(2):
        total = yr[arr, 0].astype(F32) + yr[arr, 1].astype(F32) + yr[arr, 2].astype(F32)
        acts[arr] = (total + yr[arr, 3].astype(F32)).astype(BF16)
    for c in range(C):
        grads_arrived(c)

    for copy in sent:
        if copy is not None:
            copy.wait_send()


def place_kernel(acts, grads, mask_up, mask_down, out, gin, gwu, gwd, ku, kd):
    row, col, dp = lax.axis_index("row"), lax.axis_index("col"), lax.axis_index("dp")
    yl = col // Z
    repeat_masks(mask_up, mask_down, ku, kd)
    gin[...] = acts[0]
    out[...] = acts[1]
    for quarter in range(2):
        which = yl if quarter == 0 else 1 - yl
        for c in range(C):
            there = pl.multiple_of(which * FQ + c * FC, FC)
            mine = pl.multiple_of(dp * 2 * FQ + which * FQ + c * FC, FC)
            for i in range(6):
                keep = ku[i : i + 1, pl.ds(mine, FC)]
                rows = slice(i * 64, i * 64 + 64)
                gwu[rows, pl.ds(there, FC)] = (
                    grads[0, quarter, c, rows, :].astype(F32) * keep
                ).astype(BF16)
            turned = grads[1, quarter, c].astype(F32).T
            for i in range(FC // 64):
                keep = kd[pl.ds(mine // 64 + i, 1), :]
                gwd[pl.ds(there + i * 64, 64), :] = (
                    turned[i * 64 : i * 64 + 64, :] * keep
                ).astype(BF16)


def local(tokens, grad_out, w_up, w_down, mask_up, mask_down):
    vmem = pl.BlockSpec(memory_space=pltpu.VMEM)
    hbm = pl.BlockSpec(memory_space=pl.ANY)
    keeps = [pltpu.VMEM((6, 4 * FQ), F32), pltpu.VMEM((48, DW), F32)]
    acts, grads = pl.pallas_call(
        kernel,
        out_shape=(
            jax.ShapeDtypeStruct((2, ROWS, DW), BF16),
            jax.ShapeDtypeStruct((2, 2, C, DW, FC), BF16),
        ),
        in_specs=[vmem, vmem, hbm, hbm, vmem, vmem],
        out_specs=(vmem, vmem),
        scratch_shapes=[
            *keeps,
            pltpu.VMEM((2, ROWS, DW), BF16),
            pltpu.VMEM((TOK, D2), BF16),
            pltpu.VMEM((D2, TOK), BF16),
            pltpu.VMEM((DW, FQ), BF16),
            pltpu.VMEM((2, DW, FQ), BF16),
            pltpu.VMEM((FQ, DW), BF16),
            pltpu.VMEM((2, FQ, DW), BF16),
            pltpu.VMEM((C, 2, D2, FC), BF16),
            pltpu.VMEM((C, 2, FC, D2), BF16),
            pltpu.VMEM((C, 2, DW, FC), BF16),
            pltpu.VMEM((C, 2, 2, DW, 128), BF16),
            pltpu.VMEM((C, 2, TOK, FC), F32),
            pltpu.VMEM((C, 2, 2, TB, FC), BF16),
            pltpu.VMEM((C, 2, 2, 4, TB, FC), BF16),
            pltpu.VMEM((C, 2, TB, FC), F32),
            pltpu.VMEM((C, 2, TB, FC), F32),
            pltpu.VMEM((C, 2, TOK, FC), BF16),
            pltpu.VMEM((TOK, D2), F32),
            pltpu.VMEM((6, 128, D2), BF16),
            pltpu.VMEM((6, 128, D2), BF16),
            pltpu.VMEM((256, D2), F32),
            pltpu.VMEM((4, 2, ROWS, DW), BF16),
            pltpu.VMEM((2, 4, ROWS, DW), BF16),
            pltpu.VMEM((C, 2, DW, FC), BF16),
            pltpu.VMEM((C, 2, DW, FC), BF16),
            pltpu.SemaphoreType.DMA((8,)),
            pltpu.SemaphoreType.DMA((SENDS,)),
            pltpu.SemaphoreType.DMA((MESSAGES,)),
        ],
        compiler_params=pltpu.CompilerParams(
            collective_id=0, has_side_effects=True, vmem_limit_bytes=56 * 1024 * 1024
        ),
        cost_estimate=pl.CostEstimate(
            flops=12 * TOK * D2 * FQ, bytes_accessed=8 * 1024 * 1024, transcendentals=TB * FQ
        ),
    )(tokens, grad_out, w_up, w_down, mask_up, mask_down.T)
    return pl.pallas_call(
        place_kernel,
        out_shape=(
            jax.ShapeDtypeStruct((ROWS, DW), BF16),
            jax.ShapeDtypeStruct((ROWS, DW), BF16),
            jax.ShapeDtypeStruct((DW, 2 * FQ), BF16),
            jax.ShapeDtypeStruct((2 * FQ, DW), BF16),
        ),
        in_specs=[vmem] * 4,
        out_specs=(vmem,) * 4,
        scratch_shapes=keeps,
        compiler_params=pltpu.CompilerParams(vmem_limit_bytes=60 * 1024 * 1024),
    )(acts, grads, mask_up, mask_down.T)


def solution(mesh):
    in_specs = (
        P(("row", "dp"), "col"),
        P(("row", "dp"), "col"),
        P("col", "row"),
        P("row", "col"),
        P("col", "row"),
        P("row", "col"),
    )
    out_specs = (
        P(("row", "dp"), "col"),
        P(("row", "dp"), "col"),
        P("col", ("row", "dp")),
        P(("row", "dp"), "col"),
    )
    return jax.shard_map(local, mesh=mesh, in_specs=in_specs, out_specs=out_specs, check_vma=False)
```

```python
import jax
import jax.numpy as jnp
from jax import lax
from jax.experimental import pallas as pl
from jax.experimental.pallas import tpu as pltpu
from jax.sharding import PartitionSpec as P

BLOCK = 64
MESH = pl.DeviceIdType.MESH
F32 = jnp.float32
BF16 = jnp.bfloat16

COEF_ROOT = 0.7978845608028654
COEF_CUBE = 0.044715

TOK = 1024
ROWS = 64
DW = 384
D2 = 2 * DW
FQ = 768
C = 3
FC = FQ // C
Z = 8
TB = TOK // Z
MESSAGES = 140
F2 = 2 * FC
SENDS = 40


def gelu_pair(pre_act):
    argument = COEF_ROOT * (pre_act + COEF_CUBE * pre_act * pre_act * pre_act)
    tangent = jnp.tanh(argument)
    activated = 0.5 * pre_act * (1.0 + tangent)
    gelu_slope = 0.5 * (1.0 + tangent) + 0.5 * pre_act * (1.0 - tangent * tangent) * COEF_ROOT * (
        1.0 + 3.0 * COEF_CUBE * pre_act * pre_act
    )
    return (activated, gelu_slope)


def dot_nn(a, b):
    return lax.dot_general(a, b, (((1,), (0,)), ((), ())), preferred_element_type=F32)


def dot_nt(a, b):
    return lax.dot_general(a, b, (((1,), (1,)), ((), ())), preferred_element_type=F32)


def dot_tn(a, b):
    return lax.dot_general(a, b, (((0,), (0,)), ((), ())), preferred_element_type=F32)


def repeat_masks(mask_up, mask_down, keep_up, keep_down):
    def spread(rows, cols):
        block = lax.broadcasted_iota(jnp.int32, (rows, cols), 0)
        entry = lax.broadcasted_iota(jnp.int32, (rows, cols), 1)
        return jnp.where((entry >> 6) == block, 1.0, 0.0).astype(BF16)

    keep_up[...] = dot_nn(mask_up[...].astype(F32).astype(BF16), spread(mask_up.shape[1], keep_up.shape[1]))
    keep_down[...] = dot_tn(
        mask_down[...].astype(F32).astype(BF16), spread(mask_down.shape[0], keep_down.shape[1])
    )


def kernel(
    tok, grad, wu, wd, mask_up, mask_down, acts, gwu, gwd,
    ku, kd, stage, x_all, x_turned, raw_u, raw_un, raw_d, raw_dn, w_all, w_turned, w_own, w_near,
    part, first, came, swap_s, swap_r, hid, hid_far, acc, xs, xr, yfull, ys, yr, g_own, g_sib,
    load_sem, send_sem, recv_sem,
):
    row, col, dp = lax.axis_index("row"), lax.axis_index("col"), lax.axis_index("dp")
    x, core = row // 2, row % 2
    yl, z = col // Z, col % Z
    y = dp * 2 + yl

    def at_y(v, k=None):
        v = v % 4
        place = {"col": (v % 2) * Z + z, "dp": v // 2}
        return place if k is None else {"row": x * 2 + k, **place}

    def at_x(v, k=None):
        return {"row": (v % 4) * 2 + (core if k is None else k)}

    def at_z(v):
        return {"col": yl * Z + v % Z}

    sibling = {"row": x * 2 + (1 - core)}
    y_next = (at_y(y + 1), at_y(y + 3))
    x_next = (at_x(x + 1), at_x(x + 3))
    z_next = (at_z(z + 1), at_z(z + Z - 1))

    core_at = pl.multiple_of(core * FC, FC)
    other_at = pl.multiple_of((1 - core) * FC, FC)
    partner = {"col": (1 - yl) * Z + z}

    count = [0, 0]
    sent = [None] * SENDS

    def slot(n=1):
        count[0] += n
        return count[0] - n

    def send(src, dst, device, to=None):
        at = count[1] % SENDS
        count[1] += 1
        if sent[at] is not None:
            sent[at].wait_send()
        copy = pltpu.make_async_remote_copy(
            src_ref=src, dst_ref=dst, send_sem=send_sem.at[at],
            recv_sem=recv_sem.at[slot() if to is None else to],
            device_id=device, device_id_type=MESH,
        )
        copy.start()
        sent[at] = copy
        return copy

    def arrived(ref, at):
        pltpu.make_async_remote_copy(
            src_ref=ref, dst_ref=ref, send_sem=send_sem.at[0], recv_sem=recv_sem.at[at],
            device_id=sibling, device_id_type=MESH,
        ).wait_recv()

    own_f = pl.multiple_of(y * FQ, FQ)
    near_f = [pl.multiple_of(((y + 1) % 4) * FQ, FQ), pl.multiple_of(((y + 3) % 4) * FQ, FQ)]
    loads = []

    def load(src, dst):
        copy = pltpu.make_async_copy(src, dst, load_sem.at[len(loads)])
        copy.start()
        loads.append(copy)

    for way in range(2):
        load(wu.at[:, pl.ds(near_f[way], FQ)], raw_un.at[way])
        load(wd.at[pl.ds(near_f[way], FQ), :], raw_dn.at[way])
    load(wu.at[:, pl.ds(own_f, FQ)], raw_u)
    load(wd.at[pl.ds(own_f, FQ), :], raw_d)

    barrier = pltpu.get_barrier_semaphore()
    greeted = [sibling, *z_next]
    greeted += [at_y(y + d, k) for d in (1, 2, 3) for k in (0, 1)]
    greeted += [at_x(x + d, k) for d in (1, 2, 3) for k in (0, 1)]
    for other in greeted:
        pl.semaphore_signal(barrier, inc=1, device_id=other, device_id_type=MESH)

    def block(xv, r, p, half):
        at = pl.multiple_of(p * 512 + (xv % 4) * 128 + r * ROWS, ROWS)
        return x_all.at[pl.ds(at, ROWS), pl.ds(pl.multiple_of(half * DW, DW), DW)]

    stage[0] = tok[...]
    stage[1] = grad[...]
    own_rows = pl.multiple_of(dp * 512 + row * ROWS, ROWS)
    x_all[pl.ds(own_rows, ROWS), 0:DW] = stage[core]
    pl.semaphore_wait(barrier, len(greeted))

    swap = send(stage.at[1 - core], block(x, core, dp, 0), sibling)
    first_trip = {}
    for d in (1, 3, 2):
        base = slot(2)
        first_trip[d] = base
        to_x, to_y = (x + core * d) % 4, (y + (1 - core) * d) % 4
        for arr in range(2):
            send(
                stage.at[arr],
                block(x, core, dp, (1 - core) * (d % 2)),
                {"row": to_x * 2 + arr, "col": (to_y % 2) * Z + z, "dp": to_y // 2},
                base + core,
            )
    repeat_masks(mask_up, mask_down, ku, kd)

    def trip_in(d):
        for r in range(2):
            arrived(block(x, r, dp, 0), first_trip[d] + r)

    before, after = ((y + 3) % 4) // 2, ((y + 1) % 4) // 2
    near_x, near_y, onward = {}, {}, []

    def send_x(name, p, half):
        near_x[name] = [
            send(block(x, 0, p, half), block(x, 0, p, half), x_next[way]) for way in range(2)
        ]

    def send_y(d):
        near_y[d] = [
            send(block(x + d, 1, dp, 0), block(x + d, 1, dp, 1), y_next[way]) for way in range(2)
        ]

    def on_x(name, p, half, way):
        for copy in near_x[name]:
            copy.wait_recv()
        there = x + 3 if way == 0 else x + 1
        onward.append(send(block(there, 0, p, half), block(there, 0, p, half), x_next[way]))

    def on_y(d, way):
        for copy in near_y[d]:
            copy.wait_recv()
        p = before if way == 0 else after
        onward.append(send(block(x + d, 1, p, 1), block(x + d, 1, p, 0), y_next[way]))

    near_slots = {}

    def near_weights(c):
        for way in range(2):
            f_at = c * FC + way * 128
            for i in range(6):
                keep = ku[i : i + 1, pl.ds(near_f[way] + f_at, 128)]
                w_near[c, way, 0, i * 64 : i * 64 + 64, :] = (
                    raw_un[way, i * 64 : i * 64 + 64, f_at : f_at + 128].astype(F32) * keep
                ).astype(BF16)
            rows = []
            for i in range(2):
                keep = kd[pl.ds(near_f[way] // 64 + f_at // 64 + i, 1), :]
                rows.append(raw_dn[way, f_at + i * 64 : f_at + i * 64 + 64, :].astype(F32) * keep)
            w_near[c, way, 1] = jnp.concatenate(rows, 0).T.astype(BF16)

    def send_weights(c):
        for way in range(2):
            base = slot(2)
            near_slots[c, way] = base
            for arr in range(2):
                send(
                    w_near.at[c, way, arr],
                    w_all.at[c, pl.ds(DW, DW), pl.ds(core_at + way * 128, 128)],
                    at_y(y + (1 if way == 0 else 3), arr),
                    base + core,
                )

    own_in = {}

    def own_weights(c):
        for i in range(6):
            keep = ku[i : i + 1, pl.ds(own_f + c * FC, FC)]
            w_own[c, 0, i * 64 : i * 64 + 64, :] = (
                raw_u[i * 64 : i * 64 + 64, c * FC : (c + 1) * FC].astype(F32) * keep
            ).astype(BF16)
        rows = []
        for i in range(FC // 64):
            at = c * FC + i * 64
            keep = kd[pl.ds(own_f // 64 + at // 64, 1), :]
            rows.append(raw_d[at : at + 64, :].astype(F32) * keep)
        w_own[c, 1] = jnp.concatenate(rows, 0).T.astype(BF16)
        own_in[c] = send(
            w_own.at[c, 1 - core], w_all.at[c, pl.ds(0, DW), pl.ds(core_at, FC)], sibling
        )
        w_all[c, 0:DW, pl.ds(core_at, FC)] = w_own[c, core]

    def weights_in(c):
        own_in[c].wait_recv()
        for way in range(2):
            for r in range(2):
                arrived(
                    w_all.at[c, pl.ds(DW, DW), pl.ds(r * FC + way * 128, 128)], near_slots[c, way] + r
                )

    swap.wait_recv()
    send_x("own", dp, 0)
    send_y(0)
    for copy in loads[:4]:
        copy.wait()
    near_weights(0)
    send_weights(0)
    trip_in(1)
    trip_in(3)
    send_x("after", after, 1)
    send_x("before", before, 1)
    send_y(1)
    send_y(3)
    trip_in(2)
    send_x("far", 1 - dp, 0)
    send_y(2)
    on_x("own", dp, 0, 0)
    on_y(0, 0)
    for copy in loads[4:]:
        copy.wait()
    own_weights(0)
    near_weights(1)
    on_x("after", after, 1, 0)
    on_y(1, 0)
    on_x("before", before, 1, 1)
    on_y(3, 1)
    on_x("far", 1 - dp, 0, 1)
    on_y(2, 1)
    send_weights(1)
    own_weights(1)
    near_weights(2)
    send_weights(2)
    own_weights(2)
    for copy in onward:
        copy.wait_recv()

    def steps_of(r, way):
        return 4 if r == way else 3

    def rows_of(j):
        return pl.ds(pl.multiple_of((j % Z) * TB, TB), TB)

    def pre_part(c):
        weights_in(c)

        def body(i, carry):
            rows = pl.ds(pl.multiple_of(i * 256, 256), 256)
            part[c, rows, :] = dot_nn(x_all[rows, :], w_all[c])
            return carry

        lax.fori_loop(0, TOK // 256, body, 0)

    ring = {}
    half = [slice(0, FC), slice(FC, F2)]

    def reduce_step(c, s):
        for way in range(2):
            if s > 0:
                ring[c, way, s - 1].wait_recv()
            src = came.at[c, way, s - 1] if s > 0 else first.at[c, way]
            for r in range(2):
                n = steps_of(r, way)
                if s >= n:
                    continue
                dest = z + (n - s) if way == 0 else z + Z - (n - s)
                term = part[c, rows_of(dest), half[r]]
                if s > 0:
                    term = src[:, half[r]].astype(F32) + term
                src[:, half[r]] = term.astype(BF16)
            dst = came.at[c, way, s]
            if s == 3:
                src, dst = src.at[:, pl.ds(way * FC, FC)], dst.at[:, pl.ds(way * FC, FC)]
            ring[c, way, s] = send(src, dst, z_next[way])

    swaps = {}

    def finish(c):
        for way in range(2):
            ring[c, way, 3].wait_recv()
        for r in range(2):
            value = part[c, rows_of(z), half[r]]
            for way in range(2):
                value = value + came[c, way, steps_of(r, way) - 1, :, half[r]].astype(F32)
            swap_s[c, :, half[r]] = value
        swaps[c] = send(swap_s.at[c], swap_r.at[c], sibling)

    gather, across_y = {}, {}

    def activate(c):
        swaps[c].wait_recv()
        mine, theirs = swap_s[c], swap_r[c]
        pre_act = jnp.where(core == 0, mine, theirs)
        grad_hidden = jnp.where(core == 0, theirs, mine)
        activated, slope = gelu_pair(pre_act)
        value = jnp.where(core == 0, grad_hidden * slope, activated)
        hid[c, rows_of(z), :] = value.astype(BF16)

    def to_partner(c, source, n):
        across_y[c, n] = send(hid.at[c, rows_of(source), :], hid_far.at[c, rows_of(source), :], partner)

    def gather_step(c, s):
        if s > 0:
            for way in range(2):
                gather[c, way, s - 1].wait_recv()
        for way in range(2):
            source = z + Z - s if way == 0 else z + s
            lanes = pl.ds(0, F2) if s < 3 else pl.ds(way * FC, FC)
            block_of = hid.at[c, rows_of(source), lanes]
            gather[c, way, s] = send(block_of, block_of, z_next[way])
        if s == 0:
            to_partner(c, z, 0)
        else:
            to_partner(c, z + Z - s, 2 * s - 1)
            to_partner(c, z + s, 2 * s)

    def gather_end(c):
        for way in range(2):
            gather[c, way, 3].wait_recv()
        to_partner(c, z + 4, 7)

    def turn_tokens():
        for i in range(8):
            x_turned[:, i * 128 : i * 128 + 128] = x_all[i * 128 : i * 128 + 128, 0:DW].T

    def turn_weights(c):
        w_turned[c] = w_all[c].T

    scale = float(TOK) ** -0.5
    grads_in = {}

    def weight_grads(c):
        for near_y in range(2):
            if near_y == 1:
                for n in range(8):
                    across_y[c, n].wait_recv()
            there = hid if near_y == 0 else hid_far

            def body(i, carry):
                rows = pl.ds(pl.multiple_of(i * 128, 128), 128)
                g = dot_nn(x_turned[rows, :], there[c]) * scale
                g_own[c, near_y, rows, :] = g.astype(BF16)
                return carry

            lax.fori_loop(0, DW // 128, body, 0)
            grads_in[c, near_y] = send(
                g_own.at[c, near_y, :, pl.ds(other_at, FC)], g_sib.at[c, near_y], sibling
            )

    def place(c):
        for near_y in range(2):
            grads_in[c, near_y].wait_recv()
            which = yl if near_y == 0 else 1 - yl
            there = pl.multiple_of(which * FQ + c * FC, FC)
            mine = pl.multiple_of(dp * 2 * FQ + which * FQ + c * FC, FC)
            own, sib = g_own[c, near_y, :, pl.ds(core_at, FC)], g_sib[c, near_y]
            up = jnp.where(core == 0, own.astype(F32), sib.astype(F32))
            down = jnp.where(core == 0, sib.astype(F32), own.astype(F32)).T
            for i in range(6):
                keep = ku[i : i + 1, pl.ds(mine, FC)]
                gwu[i * 64 : i * 64 + 64, pl.ds(there, FC)] = (
                    up[i * 64 : i * 64 + 64, :] * keep
                ).astype(BF16)
            for i in range(FC // 64):
                keep = kd[pl.ds(mine // 64 + i, 1), :]
                gwd[pl.ds(there + i * 64, 64), :] = (down[i * 64 : i * 64 + 64, :] * keep).astype(BF16)

    def act_part(c):
        def body(i, carry):
            rows = pl.ds(pl.multiple_of(i * 256, 256), 256)
            o = dot_nn(hid[c, rows, :], w_turned[c])
            acc[rows, :] = o if c == 0 else o + acc[rows, :]
            return carry

        lax.fori_loop(0, TOK // 256, body, 0)

    pre_part(0)
    reduce_step(0, 0)
    pre_part(1)
    reduce_step(1, 0)
    reduce_step(0, 1)
    turn_tokens()
    reduce_step(1, 1)
    reduce_step(0, 2)
    pre_part(2)
    reduce_step(2, 0)
    turn_weights(0)
    reduce_step(0, 3)
    reduce_step(1, 2)
    reduce_step(2, 1)
    finish(0)
    turn_weights(1)
    activate(0)
    gather_step(0, 0)
    reduce_step(1, 3)
    reduce_step(2, 2)
    gather_step(0, 1)
    finish(1)
    turn_weights(2)
    reduce_step(2, 3)
    activate(1)
    gather_step(1, 0)
    gather_step(0, 2)
    finish(2)
    activate(2)
    gather_step(2, 0)
    gather_step(0, 3)
    gather_step(1, 1)
    gather_step(2, 1)
    gather_step(1, 2)
    gather_end(0)
    gather_step(2, 2)
    act_part(0)
    gather_step(1, 3)
    weight_grads(0)
    gather_step(2, 3)
    gather_end(1)
    act_part(1)
    gather_end(2)
    act_part(2)

    def x_term(xv, p):
        return acc[pl.ds(pl.multiple_of(p * 512 + (xv % 4) * 128, 128), 128), :]

    def x_send(at, value, way):
        xs[at] = value.astype(BF16)
        return send(xs.at[at], xr.at[at], x_next[way])

    r0 = x_send(0, x_term(x + 2, 0), 0)
    l0 = x_send(1, x_term(x + 2, 1), 1)
    r1b = x_send(2, x_term(x + 1, 1), 0)
    l1a = x_send(3, x_term(x + 3, 0), 1)
    weight_grads(1)
    r0.wait_recv()
    r1a = x_send(4, x_term(x + 1, 0) + xr[0].astype(F32), 0)
    l0.wait_recv()
    l1b = x_send(5, x_term(x + 3, 1) + xr[1].astype(F32), 1)
    weight_grads(2)
    place(0)
    place(1)
    for copy in (r1b, l1a, r1a, l1b):
        copy.wait_recv()
    yfull[0:128, :] = x_term(x, 0) + xr[4].astype(F32) + xr[3].astype(F32)
    yfull[128:256, :] = x_term(x, 1) + xr[2].astype(F32) + xr[5].astype(F32)

    def y_term(half, r, p):
        at = pl.multiple_of(p * 128 + r * ROWS, ROWS)
        return yfull[pl.ds(at, ROWS), half * DW : half * DW + DW].astype(BF16)

    last = []
    for d, half, p in ((2, 0, 1 - dp), (1, 1, after), (3, 1, before)):
        base = slot(2)
        last.append((d, base))
        for r in range(2):
            ys[d, r] = y_term(half, r, p)
            send(ys.at[d, r], yr.at[core, d], at_y(y + d, r), base + core)
    ys[0, 0] = y_term(0, 1 - core, dp)
    across = send(ys.at[0, 0], yr.at[core, 0], sibling)
    yr[core, 0] = y_term(0, core, dp)
    place(2)
    for d, base in last:
        for arr in range(2):
            arrived(yr.at[arr, d], base + arr)
    across.wait_recv()
    for arr in range(2):
        total = yr[arr, 0].astype(F32) + yr[arr, 1].astype(F32) + yr[arr, 2].astype(F32)
        acts[arr] = (total + yr[arr, 3].astype(F32)).astype(BF16)

    for copy in sent:
        if copy is not None:
            copy.wait_send()


def place_kernel(acts, gwu, gwd, out, gin, gwu_out, gwd_out, sems):
    moves = ((acts.at[1], out), (acts.at[0], gin), (gwu, gwu_out), (gwd, gwd_out))
    copies = [pltpu.make_async_copy(src, dst, sems.at[i]) for i, (src, dst) in enumerate(moves)]
    for copy in copies:
        copy.start()
    for copy in copies:
        copy.wait()


def local(tokens, grad_out, w_up, w_down, mask_up, mask_down):
    vmem = pl.BlockSpec(memory_space=pltpu.VMEM)
    hbm = pl.BlockSpec(memory_space=pl.ANY)
    keeps = [pltpu.VMEM((6, 4 * FQ), F32), pltpu.VMEM((48, DW), F32)]
    acts, grad_up, grad_down = pl.pallas_call(
        kernel,
        out_shape=(
            jax.ShapeDtypeStruct((2, ROWS, DW), BF16),
            jax.ShapeDtypeStruct((DW, 2 * FQ), BF16),
            jax.ShapeDtypeStruct((2 * FQ, DW), BF16),
        ),
        in_specs=[vmem, vmem, hbm, hbm, vmem, vmem],
        out_specs=(vmem, vmem, vmem),
        scratch_shapes=[
            *keeps,
            pltpu.VMEM((2, ROWS, DW), BF16),
            pltpu.VMEM((TOK, D2), BF16),
            pltpu.VMEM((DW, TOK), BF16),
            pltpu.VMEM((DW, FQ), BF16),
            pltpu.VMEM((2, DW, FQ), BF16),
            pltpu.VMEM((FQ, DW), BF16),
            pltpu.VMEM((2, FQ, DW), BF16),
            pltpu.VMEM((C, D2, F2), BF16),
            pltpu.VMEM((C, F2, D2), BF16),
            pltpu.VMEM((C, 2, DW, FC), BF16),
            pltpu.VMEM((C, 2, 2, DW, 128), BF16),
            pltpu.VMEM((C, TOK, F2), F32),
            pltpu.VMEM((C, 2, TB, F2), BF16),
            pltpu.VMEM((C, 2, 4, TB, F2), BF16),
            pltpu.VMEM((C, TB, F2), F32),
            pltpu.VMEM((C, TB, F2), F32),
            pltpu.VMEM((C, TOK, F2), BF16),
            pltpu.VMEM((C, TOK, F2), BF16),
            pltpu.VMEM((TOK, D2), F32),
            pltpu.VMEM((6, 128, D2), BF16),
            pltpu.VMEM((6, 128, D2), BF16),
            pltpu.VMEM((256, D2), F32),
            pltpu.VMEM((4, 2, ROWS, DW), BF16),
            pltpu.VMEM((2, 4, ROWS, DW), BF16),
            pltpu.VMEM((C, 2, DW, F2), BF16),
            pltpu.VMEM((C, 2, DW, FC), BF16),
            pltpu.SemaphoreType.DMA((8,)),
            pltpu.SemaphoreType.DMA((SENDS,)),
            pltpu.SemaphoreType.DMA((MESSAGES,)),
        ],
        compiler_params=pltpu.CompilerParams(
            collective_id=0, has_side_effects=True, vmem_limit_bytes=56 * 1024 * 1024
        ),
        cost_estimate=pl.CostEstimate(
            flops=12 * TOK * D2 * FQ, bytes_accessed=8 * 1024 * 1024, transcendentals=TB * FQ
        ),
    )(tokens, grad_out, w_up, w_down, mask_up, mask_down.T)
    return pl.pallas_call(
        place_kernel,
        out_shape=(
            jax.ShapeDtypeStruct((ROWS, DW), BF16),
            jax.ShapeDtypeStruct((ROWS, DW), BF16),
            jax.ShapeDtypeStruct((DW, 2 * FQ), BF16),
            jax.ShapeDtypeStruct((2 * FQ, DW), BF16),
        ),
        in_specs=[hbm] * 3,
        out_specs=(hbm,) * 4,
        scratch_shapes=[pltpu.SemaphoreType.DMA((4,))],
        compiler_params=pltpu.CompilerParams(vmem_limit_bytes=60 * 1024 * 1024),
    )(acts, grad_up, grad_down)


def solution(mesh):
    in_specs = (
        P(("row", "dp"), "col"),
        P(("row", "dp"), "col"),
        P("col", "row"),
        P("row", "col"),
        P("col", "row"),
        P("row", "col"),
    )
    out_specs = (
        P(("row", "dp"), "col"),
        P(("row", "dp"), "col"),
        P("col", ("row", "dp")),
        P(("row", "dp"), "col"),
    )
    return jax.shard_map(local, mesh=mesh, in_specs=in_specs, out_specs=out_specs, check_vma=False)
```

```python
import jax
import jax.numpy as jnp
from jax import lax
from jax.experimental import pallas as pl
from jax.experimental.pallas import tpu as pltpu
from jax.sharding import PartitionSpec as P

BLOCK = 64
MESH = pl.DeviceIdType.MESH
F32 = jnp.float32
BF16 = jnp.bfloat16

COEF_ROOT = 0.7978845608028654
COEF_CUBE = 0.044715

TOK = 1024
ROWS = 64
DW = 384
D2 = 2 * DW
FQ = 768
C = 3
FC = FQ // C
Z = 8
TB = TOK // Z
MESSAGES = 119
F2 = 2 * FC
SENDS = 40


def gelu_pair(pre_act):
    argument = COEF_ROOT * (pre_act + COEF_CUBE * pre_act * pre_act * pre_act)
    tangent = jnp.tanh(argument)
    activated = 0.5 * pre_act * (1.0 + tangent)
    gelu_slope = 0.5 * (1.0 + tangent) + 0.5 * pre_act * (1.0 - tangent * tangent) * COEF_ROOT * (
        1.0 + 3.0 * COEF_CUBE * pre_act * pre_act
    )
    return (activated, gelu_slope)


def dot_nn(a, b):
    return lax.dot_general(a, b, (((1,), (0,)), ((), ())), preferred_element_type=F32)


def dot_nt(a, b):
    return lax.dot_general(a, b, (((1,), (1,)), ((), ())), preferred_element_type=F32)


def dot_tn(a, b):
    return lax.dot_general(a, b, (((0,), (0,)), ((), ())), preferred_element_type=F32)


def repeat_masks(mask_up, mask_down, keep_up, keep_down):
    def spread(rows, cols):
        block = lax.broadcasted_iota(jnp.int32, (rows, cols), 0)
        entry = lax.broadcasted_iota(jnp.int32, (rows, cols), 1)
        return jnp.where((entry >> 6) == block, 1.0, 0.0).astype(BF16)

    keep_up[...] = dot_nn(mask_up[...].astype(F32).astype(BF16), spread(mask_up.shape[1], keep_up.shape[1]))
    keep_down[...] = dot_tn(
        mask_down[...].astype(F32).astype(BF16), spread(mask_down.shape[0], keep_down.shape[1])
    )


def kernel(
    tok, grad, wu, wd, mask_up, mask_down, acts, gwu, gwd,
    ku, kd, stage, x_all, x_turned, raw_u, raw_un, raw_d, raw_dn, w_all, w_turned, w_own, w_near,
    part, first, came, swap_s, swap_r, hid, acc, xs, xr, yfull, ys, yr, g_own, g_far, g_sib, g_far_in,
    load_sem, send_sem, recv_sem,
):
    row, col, dp = lax.axis_index("row"), lax.axis_index("col"), lax.axis_index("dp")
    x, core = row // 2, row % 2
    yl, z = col // Z, col % Z
    y = dp * 2 + yl

    def at_y(v, k=None):
        v = v % 4
        place = {"col": (v % 2) * Z + z, "dp": v // 2}
        return place if k is None else {"row": x * 2 + k, **place}

    def at_x(v, k=None):
        return {"row": (v % 4) * 2 + (core if k is None else k)}

    def at_z(v):
        return {"col": yl * Z + v % Z}

    sibling = {"row": x * 2 + (1 - core)}
    y_next = (at_y(y + 1), at_y(y + 3))
    x_next = (at_x(x + 1), at_x(x + 3))
    z_next = (at_z(z + 1), at_z(z + Z - 1))

    core_at = pl.multiple_of(core * FC, FC)
    other_at = pl.multiple_of((1 - core) * FC, FC)

    count = [0, 0]
    sent = [None] * SENDS

    def slot(n=1):
        count[0] += n
        return count[0] - n

    def send(src, dst, device, to=None):
        at = count[1] % SENDS
        count[1] += 1
        if sent[at] is not None:
            sent[at].wait_send()
        copy = pltpu.make_async_remote_copy(
            src_ref=src, dst_ref=dst, send_sem=send_sem.at[at],
            recv_sem=recv_sem.at[slot() if to is None else to],
            device_id=device, device_id_type=MESH,
        )
        copy.start()
        sent[at] = copy
        return copy

    def arrived(ref, at):
        pltpu.make_async_remote_copy(
            src_ref=ref, dst_ref=ref, send_sem=send_sem.at[0], recv_sem=recv_sem.at[at],
            device_id=sibling, device_id_type=MESH,
        ).wait_recv()

    own_f = pl.multiple_of(y * FQ, FQ)
    near_f = [pl.multiple_of(((y + 1) % 4) * FQ, FQ), pl.multiple_of(((y + 3) % 4) * FQ, FQ)]
    loads = []

    def load(src, dst):
        copy = pltpu.make_async_copy(src, dst, load_sem.at[len(loads)])
        copy.start()
        loads.append(copy)

    for way in range(2):
        load(wu.at[:, pl.ds(near_f[way], FQ)], raw_un.at[way])
        load(wd.at[pl.ds(near_f[way], FQ), :], raw_dn.at[way])
    load(wu.at[:, pl.ds(own_f, FQ)], raw_u)
    load(wd.at[pl.ds(own_f, FQ), :], raw_d)

    barrier = pltpu.get_barrier_semaphore()
    greeted = [sibling, *z_next]
    greeted += [at_y(y + d, k) for d in (1, 2, 3) for k in (0, 1)]
    greeted += [at_x(x + d, k) for d in (1, 2, 3) for k in (0, 1)]
    for other in greeted:
        pl.semaphore_signal(barrier, inc=1, device_id=other, device_id_type=MESH)

    def block(xv, r, p, half):
        at = pl.multiple_of(p * 512 + (xv % 4) * 128 + r * ROWS, ROWS)
        return x_all.at[pl.ds(at, ROWS), pl.ds(pl.multiple_of(half * DW, DW), DW)]

    stage[0] = tok[...]
    stage[1] = grad[...]
    own_rows = pl.multiple_of(dp * 512 + row * ROWS, ROWS)
    x_all[pl.ds(own_rows, ROWS), 0:DW] = stage[core]
    pl.semaphore_wait(barrier, len(greeted))

    swap = send(stage.at[1 - core], block(x, core, dp, 0), sibling)
    first_trip = {}
    for d in (1, 3, 2):
        base = slot(2)
        first_trip[d] = base
        to_x, to_y = (x + core * d) % 4, (y + (1 - core) * d) % 4
        for arr in range(2):
            send(
                stage.at[arr],
                block(x, core, dp, (1 - core) * (d % 2)),
                {"row": to_x * 2 + arr, "col": (to_y % 2) * Z + z, "dp": to_y // 2},
                base + core,
            )
    repeat_masks(mask_up, mask_down, ku, kd)

    def trip_in(d):
        for r in range(2):
            arrived(block(x, r, dp, 0), first_trip[d] + r)

    before, after = ((y + 3) % 4) // 2, ((y + 1) % 4) // 2
    near_x, near_y, onward = {}, {}, []

    def send_x(name, p, half):
        near_x[name] = [
            send(block(x, 0, p, half), block(x, 0, p, half), x_next[way]) for way in range(2)
        ]

    def send_y(d):
        near_y[d] = [
            send(block(x + d, 1, dp, 0), block(x + d, 1, dp, 1), y_next[way]) for way in range(2)
        ]

    def on_x(name, p, half, way):
        for copy in near_x[name]:
            copy.wait_recv()
        there = x + 3 if way == 0 else x + 1
        onward.append(send(block(there, 0, p, half), block(there, 0, p, half), x_next[way]))

    def on_y(d, way):
        for copy in near_y[d]:
            copy.wait_recv()
        p = before if way == 0 else after
        onward.append(send(block(x + d, 1, p, 1), block(x + d, 1, p, 0), y_next[way]))

    near_slots = {}

    def near_weights(c):
        for way in range(2):
            f_at = c * FC + way * 128
            for i in range(6):
                keep = ku[i : i + 1, pl.ds(near_f[way] + f_at, 128)]
                w_near[c, way, 0, i * 64 : i * 64 + 64, :] = (
                    raw_un[way, i * 64 : i * 64 + 64, f_at : f_at + 128].astype(F32) * keep
                ).astype(BF16)
            rows = []
            for i in range(2):
                keep = kd[pl.ds(near_f[way] // 64 + f_at // 64 + i, 1), :]
                rows.append(raw_dn[way, f_at + i * 64 : f_at + i * 64 + 64, :].astype(F32) * keep)
            w_near[c, way, 1] = jnp.concatenate(rows, 0).T.astype(BF16)

    def send_weights(c):
        for way in range(2):
            base = slot(2)
            near_slots[c, way] = base
            for arr in range(2):
                send(
                    w_near.at[c, way, arr],
                    w_all.at[c, pl.ds(DW, DW), pl.ds(core_at + way * 128, 128)],
                    at_y(y + (1 if way == 0 else 3), arr),
                    base + core,
                )

    own_in = {}

    def own_weights(c):
        for i in range(6):
            keep = ku[i : i + 1, pl.ds(own_f + c * FC, FC)]
            w_own[c, 0, i * 64 : i * 64 + 64, :] = (
                raw_u[i * 64 : i * 64 + 64, c * FC : (c + 1) * FC].astype(F32) * keep
            ).astype(BF16)
        rows = []
        for i in range(FC // 64):
            at = c * FC + i * 64
            keep = kd[pl.ds(own_f // 64 + at // 64, 1), :]
            rows.append(raw_d[at : at + 64, :].astype(F32) * keep)
        w_own[c, 1] = jnp.concatenate(rows, 0).T.astype(BF16)
        own_in[c] = send(
            w_own.at[c, 1 - core], w_all.at[c, pl.ds(0, DW), pl.ds(core_at, FC)], sibling
        )
        w_all[c, 0:DW, pl.ds(core_at, FC)] = w_own[c, core]

    def weights_in(c):
        own_in[c].wait_recv()
        for way in range(2):
            for r in range(2):
                arrived(
                    w_all.at[c, pl.ds(DW, DW), pl.ds(r * FC + way * 128, 128)], near_slots[c, way] + r
                )

    swap.wait_recv()
    send_x("own", dp, 0)
    send_y(0)
    for copy in loads[:4]:
        copy.wait()
    near_weights(0)
    send_weights(0)
    trip_in(1)
    trip_in(3)
    send_x("after", after, 1)
    send_x("before", before, 1)
    send_y(1)
    send_y(3)
    trip_in(2)
    send_x("far", 1 - dp, 0)
    send_y(2)
    on_x("own", dp, 0, 0)
    on_y(0, 0)
    for copy in loads[4:]:
        copy.wait()
    own_weights(0)
    near_weights(1)
    on_x("after", after, 1, 0)
    on_y(1, 0)
    on_x("before", before, 1, 1)
    on_y(3, 1)
    on_x("far", 1 - dp, 0, 1)
    on_y(2, 1)
    send_weights(1)
    own_weights(1)
    near_weights(2)
    send_weights(2)
    own_weights(2)
    for copy in onward:
        copy.wait_recv()

    def steps_of(r, way):
        return 4 if r == way else 3

    def rows_of(j):
        return pl.ds(pl.multiple_of((j % Z) * TB, TB), TB)

    def pre_part(c):
        weights_in(c)

        def body(i, carry):
            rows = pl.ds(pl.multiple_of(i * 256, 256), 256)
            part[c, rows, :] = dot_nn(x_all[rows, :], w_all[c])
            return carry

        lax.fori_loop(0, TOK // 256, body, 0)

    def pre_block(c, j):
        part[c, rows_of(j), :] = dot_nn(x_all[rows_of(j), :], w_all[c])

    ring = {}
    half = [slice(0, FC), slice(FC, F2)]

    def reduce_step(c, s):
        for way in range(2):
            if s > 0:
                ring[c, way, s - 1].wait_recv()
            src = came.at[c, way, s - 1] if s > 0 else first.at[c, way]
            for r in range(2):
                n = steps_of(r, way)
                if s >= n:
                    continue
                dest = z + (n - s) if way == 0 else z + Z - (n - s)
                term = part[c, rows_of(dest), half[r]]
                if s > 0:
                    term = src[:, half[r]].astype(F32) + term
                src[:, half[r]] = term.astype(BF16)
            dst = came.at[c, way, s]
            if s == 3:
                src, dst = src.at[:, pl.ds(way * FC, FC)], dst.at[:, pl.ds(way * FC, FC)]
            ring[c, way, s] = send(src, dst, z_next[way])

    swaps = {}

    def finish(c):
        for way in range(2):
            ring[c, way, 3].wait_recv()
        for r in range(2):
            value = part[c, rows_of(z), half[r]]
            for way in range(2):
                value = value + came[c, way, steps_of(r, way) - 1, :, half[r]].astype(F32)
            swap_s[c, :, half[r]] = value
        swaps[c] = send(swap_s.at[c], swap_r.at[c], sibling)

    gather = {}

    def activate(c):
        swaps[c].wait_recv()
        mine, theirs = swap_s[c], swap_r[c]
        pre_act = jnp.where(core == 0, mine, theirs)
        grad_hidden = jnp.where(core == 0, theirs, mine)
        activated, slope = gelu_pair(pre_act)
        value = jnp.where(core == 0, grad_hidden * slope, activated)
        hid[c, rows_of(z), :] = value.astype(BF16)

    def gather_step(c, s):
        if s > 0:
            for way in range(2):
                gather[c, way, s - 1].wait_recv()
        for way in range(2):
            source = z + Z - s if way == 0 else z + s
            lanes = pl.ds(0, F2) if s < 3 else pl.ds(way * FC, FC)
            block_of = hid.at[c, rows_of(source), lanes]
            gather[c, way, s] = send(block_of, block_of, z_next[way])

    def gather_end(c):
        for way in range(2):
            gather[c, way, 3].wait_recv()

    def turn_tokens():
        for i in range(8):
            x_turned[:, i * 128 : i * 128 + 128] = x_all[i * 128 : i * 128 + 128, :].T

    def turn_weights(c):
        w_turned[c] = w_all[c].T

    scale = float(TOK) ** -0.5
    grads_in = {}

    def weight_grads(c):
        def width(dst, first_row):
            def body(i, carry):
                rows = pl.ds(pl.multiple_of(i * 128, 128), 128)
                wide = pl.ds(pl.multiple_of(first_row + i * 128, 128), 128)
                dst[c, rows, :] = (dot_nn(x_turned[wide, :], hid[c]) * scale).astype(BF16)
                return carry

            lax.fori_loop(0, DW // 128, body, 0)

        width(g_far, DW)
        base = slot(2)
        for r in range(2):
            send(
                g_far.at[c, :, pl.ds(r * FC, FC)], g_far_in.at[core, c],
                at_y(y + 1 - 2 * yl, r), base + core,
            )
        width(g_own, 0)
        across = send(g_own.at[c, :, pl.ds(other_at, FC)], g_sib.at[c], sibling)
        grads_in[c] = (across, base)

    def place(c, which, up, down):
        there = pl.multiple_of(which * FQ + c * FC, FC)
        mine = pl.multiple_of(dp * 2 * FQ + which * FQ + c * FC, FC)
        for i in range(6):
            keep = ku[i : i + 1, pl.ds(mine, FC)]
            gwu[i * 64 : i * 64 + 64, pl.ds(there, FC)] = (
                up[i * 64 : i * 64 + 64, :] * keep
            ).astype(BF16)
        down = down.T
        for i in range(FC // 64):
            keep = kd[pl.ds(mine // 64 + i, 1), :]
            gwd[pl.ds(there + i * 64, 64), :] = (down[i * 64 : i * 64 + 64, :] * keep).astype(BF16)

    def place_own(c):
        grads_in[c][0].wait_recv()
        own, sib = g_own[c, :, pl.ds(core_at, FC)].astype(F32), g_sib[c].astype(F32)
        place(c, yl, jnp.where(core == 0, own, sib), jnp.where(core == 0, sib, own))

    def place_far(c):
        for arr in range(2):
            arrived(g_far_in.at[arr, c], grads_in[c][1] + arr)
        place(c, 1 - yl, g_far_in[0, c].astype(F32), g_far_in[1, c].astype(F32))

    def act_part(c):
        def body(i, carry):
            rows = pl.ds(pl.multiple_of(i * 256, 256), 256)
            o = dot_nn(hid[c, rows, :], w_turned[c])
            acc[rows, :] = o if c == 0 else o + acc[rows, :]
            return carry

        lax.fori_loop(0, TOK // 256, body, 0)

    weights_in(0)
    for j in (z + 4, z + 3, z + 5):
        pre_block(0, j)
    reduce_step(0, 0)
    for j in (z + 2, z + 6, z + 1, z + 7, z):
        pre_block(0, j)
    pre_part(1)
    reduce_step(1, 0)
    reduce_step(0, 1)
    turn_tokens()
    reduce_step(1, 1)
    reduce_step(0, 2)
    pre_part(2)
    reduce_step(2, 0)
    turn_weights(0)
    reduce_step(0, 3)
    reduce_step(1, 2)
    reduce_step(2, 1)
    finish(0)
    turn_weights(1)
    activate(0)
    gather_step(0, 0)
    reduce_step(1, 3)
    reduce_step(2, 2)
    gather_step(0, 1)
    finish(1)
    turn_weights(2)
    reduce_step(2, 3)
    activate(1)
    gather_step(1, 0)
    gather_step(0, 2)
    finish(2)
    activate(2)
    gather_step(2, 0)
    gather_step(0, 3)
    gather_step(1, 1)
    gather_step(2, 1)
    gather_step(1, 2)
    gather_end(0)
    weight_grads(0)
    gather_step(2, 2)
    gather_step(1, 3)
    act_part(0)
    gather_step(2, 3)
    gather_end(1)
    weight_grads(1)
    act_part(1)
    gather_end(2)

    def x_rows(xv, p):
        return pl.ds(pl.multiple_of(p * 512 + (xv % 4) * 128, 128), 128)

    def x_first(xv, p):
        rows = x_rows(xv, p)
        return acc[rows, :] + dot_nn(hid[2, rows, :], w_turned[2])

    def x_term(xv, p):
        return acc[x_rows(xv, p), :]

    def x_send(at, value, way):
        xs[at] = value.astype(BF16)
        return send(xs.at[at], xr.at[at], x_next[way])

    r0 = x_send(0, x_first(x + 2, 0), 0)
    l0 = x_send(1, x_first(x + 2, 1), 1)
    r1b = x_send(2, x_first(x + 1, 1), 0)
    l1a = x_send(3, x_first(x + 3, 0), 1)
    for xv, p in ((x + 1, 0), (x + 3, 1), (x, 0), (x, 1)):
        acc[x_rows(xv, p), :] = x_first(xv, p)
    weight_grads(2)
    place_own(0)
    r0.wait_recv()
    r1a = x_send(4, x_term(x + 1, 0) + xr[0].astype(F32), 0)
    l0.wait_recv()
    l1b = x_send(5, x_term(x + 3, 1) + xr[1].astype(F32), 1)
    place_far(0)
    place_own(1)
    place_own(2)
    for copy in (r1b, l1a, r1a, l1b):
        copy.wait_recv()
    yfull[0:128, :] = x_term(x, 0) + xr[4].astype(F32) + xr[3].astype(F32)
    yfull[128:256, :] = x_term(x, 1) + xr[2].astype(F32) + xr[5].astype(F32)

    def y_term(half, r, p):
        at = pl.multiple_of(p * 128 + r * ROWS, ROWS)
        return yfull[pl.ds(at, ROWS), half * DW : half * DW + DW].astype(BF16)

    last = []
    for d, half, p in ((2, 0, 1 - dp), (1, 1, after), (3, 1, before)):
        base = slot(2)
        last.append((d, base))
        for r in range(2):
            ys[d, r] = y_term(half, r, p)
            send(ys.at[d, r], yr.at[core, d], at_y(y + d, r), base + core)
    ys[0, 0] = y_term(0, 1 - core, dp)
    across = send(ys.at[0, 0], yr.at[core, 0], sibling)
    yr[core, 0] = y_term(0, core, dp)
    place_far(1)
    place_far(2)
    for d, base in last:
        for arr in range(2):
            arrived(yr.at[arr, d], base + arr)
    across.wait_recv()
    for arr in range(2):
        total = yr[arr, 0].astype(F32) + yr[arr, 1].astype(F32) + yr[arr, 2].astype(F32)
        acts[arr] = (total + yr[arr, 3].astype(F32)).astype(BF16)

    for copy in sent:
        if copy is not None:
            copy.wait_send()


def place_kernel(acts, gwu, gwd, out, gin, gwu_out, gwd_out):
    gin[...] = acts[0]
    out[...] = acts[1]
    gwu_out[...] = gwu[...]
    gwd_out[...] = gwd[...]


def local(tokens, grad_out, w_up, w_down, mask_up, mask_down):
    vmem = pl.BlockSpec(memory_space=pltpu.VMEM)
    hbm = pl.BlockSpec(memory_space=pl.ANY)
    keeps = [pltpu.VMEM((6, 4 * FQ), F32), pltpu.VMEM((48, DW), F32)]
    acts, grad_up, grad_down = pl.pallas_call(
        kernel,
        out_shape=(
            jax.ShapeDtypeStruct((2, ROWS, DW), BF16),
            jax.ShapeDtypeStruct((DW, 2 * FQ), BF16),
            jax.ShapeDtypeStruct((2 * FQ, DW), BF16),
        ),
        in_specs=[vmem, vmem, hbm, hbm, vmem, vmem],
        out_specs=(vmem, vmem, vmem),
        scratch_shapes=[
            *keeps,
            pltpu.VMEM((2, ROWS, DW), BF16),
            pltpu.VMEM((TOK, D2), BF16),
            pltpu.VMEM((D2, TOK), BF16),
            pltpu.VMEM((DW, FQ), BF16),
            pltpu.VMEM((2, DW, FQ), BF16),
            pltpu.VMEM((FQ, DW), BF16),
            pltpu.VMEM((2, FQ, DW), BF16),
            pltpu.VMEM((C, D2, F2), BF16),
            pltpu.VMEM((C, F2, D2), BF16),
            pltpu.VMEM((C, 2, DW, FC), BF16),
            pltpu.VMEM((C, 2, 2, DW, 128), BF16),
            pltpu.VMEM((C, TOK, F2), F32),
            pltpu.VMEM((C, 2, TB, F2), BF16),
            pltpu.VMEM((C, 2, 4, TB, F2), BF16),
            pltpu.VMEM((C, TB, F2), F32),
            pltpu.VMEM((C, TB, F2), F32),
            pltpu.VMEM((C, TOK, F2), BF16),
            pltpu.VMEM((TOK, D2), F32),
            pltpu.VMEM((6, 128, D2), BF16),
            pltpu.VMEM((6, 128, D2), BF16),
            pltpu.VMEM((256, D2), F32),
            pltpu.VMEM((4, 2, ROWS, DW), BF16),
            pltpu.VMEM((2, 4, ROWS, DW), BF16),
            pltpu.VMEM((C, DW, F2), BF16),
            pltpu.VMEM((C, DW, F2), BF16),
            pltpu.VMEM((C, DW, FC), BF16),
            pltpu.VMEM((2, C, DW, FC), BF16),
            pltpu.SemaphoreType.DMA((8,)),
            pltpu.SemaphoreType.DMA((SENDS,)),
            pltpu.SemaphoreType.DMA((MESSAGES,)),
        ],
        compiler_params=pltpu.CompilerParams(
            collective_id=0, has_side_effects=True, vmem_limit_bytes=56 * 1024 * 1024
        ),
        cost_estimate=pl.CostEstimate(
            flops=12 * TOK * D2 * FQ, bytes_accessed=8 * 1024 * 1024, transcendentals=TB * FQ
        ),
    )(tokens, grad_out, w_up, w_down, mask_up, mask_down.T)
    return pl.pallas_call(
        place_kernel,
        out_shape=(
            jax.ShapeDtypeStruct((ROWS, DW), BF16),
            jax.ShapeDtypeStruct((ROWS, DW), BF16),
            jax.ShapeDtypeStruct((DW, 2 * FQ), BF16),
            jax.ShapeDtypeStruct((2 * FQ, DW), BF16),
        ),
        in_specs=[vmem] * 3,
        out_specs=(vmem,) * 4,
        compiler_params=pltpu.CompilerParams(vmem_limit_bytes=60 * 1024 * 1024),
    )(acts, grad_up, grad_down)


def solution(mesh):
    in_specs = (
        P(("row", "dp"), "col"),
        P(("row", "dp"), "col"),
        P("col", "row"),
        P("row", "col"),
        P("col", "row"),
        P("row", "col"),
    )
    out_specs = (
        P(("row", "dp"), "col"),
        P(("row", "dp"), "col"),
        P("col", ("row", "dp")),
        P(("row", "dp"), "col"),
    )
    return jax.shard_map(local, mesh=mesh, in_specs=in_specs, out_specs=out_specs, check_vma=False)
```

```python
import jax
import jax.numpy as jnp
from jax import lax
from jax.experimental import pallas as pl
from jax.experimental.pallas import tpu as pltpu
from jax.sharding import PartitionSpec as P

BLOCK = 64
MESH = pl.DeviceIdType.MESH
F32 = jnp.float32
BF16 = jnp.bfloat16

COEF_ROOT = 0.7978845608028654
COEF_CUBE = 0.044715

TOK = 1024
ROWS = 64
DW = 384
D2 = 2 * DW
FQ = 768
C = 3
FC = FQ // C
Z = 8
TB = TOK // Z
MESSAGES = 119
F2 = 2 * FC
SENDS = 32


def gelu_pair(pre_act):
    argument = COEF_ROOT * (pre_act + COEF_CUBE * pre_act * pre_act * pre_act)
    tangent = jnp.tanh(argument)
    activated = 0.5 * pre_act * (1.0 + tangent)
    gelu_slope = 0.5 * (1.0 + tangent) + 0.5 * pre_act * (1.0 - tangent * tangent) * COEF_ROOT * (
        1.0 + 3.0 * COEF_CUBE * pre_act * pre_act
    )
    return (activated, gelu_slope)


def dot_nn(a, b):
    return lax.dot_general(a, b, (((1,), (0,)), ((), ())), preferred_element_type=F32)


def dot_nt(a, b):
    return lax.dot_general(a, b, (((1,), (1,)), ((), ())), preferred_element_type=F32)


def dot_tn(a, b):
    return lax.dot_general(a, b, (((0,), (0,)), ((), ())), preferred_element_type=F32)


def repeat_masks(mask_up, mask_down, keep_up, keep_down):
    def spread(rows, cols):
        block = lax.broadcasted_iota(jnp.int32, (rows, cols), 0)
        entry = lax.broadcasted_iota(jnp.int32, (rows, cols), 1)
        return jnp.where((entry >> 6) == block, 1.0, 0.0).astype(BF16)

    keep_up[...] = dot_nn(mask_up[...].astype(F32).astype(BF16), spread(mask_up.shape[1], keep_up.shape[1]))
    keep_down[...] = dot_tn(
        mask_down[...].astype(F32).astype(BF16), spread(mask_down.shape[0], keep_down.shape[1])
    )


def kernel(
    tok, grad, wu, wd, mask_up, mask_down, acts, gwu, gwd,
    ku, kd, stage, x_all, x_turned, raw_u, raw_un, raw_d, raw_dn, w_all, w_turned, w_own, w_near,
    part, first, came, swap_s, swap_r, hid, acc, xs, xr, yfull, ys, yr, g_own, g_far, g_sib, g_far_in,
    load_sem, send_sem, recv_sem,
):
    row, col, dp = lax.axis_index("row"), lax.axis_index("col"), lax.axis_index("dp")
    x, core = row // 2, row % 2
    yl, z = col // Z, col % Z
    y = dp * 2 + yl

    def at_y(v, k=None):
        v = v % 4
        place = {"col": (v % 2) * Z + z, "dp": v // 2}
        return place if k is None else {"row": x * 2 + k, **place}

    def at_x(v, k=None):
        return {"row": (v % 4) * 2 + (core if k is None else k)}

    def at_z(v):
        return {"col": yl * Z + v % Z}

    sibling = {"row": x * 2 + (1 - core)}
    y_next = (at_y(y + 1), at_y(y + 3))
    x_next = (at_x(x + 1), at_x(x + 3))
    z_next = (at_z(z + 1), at_z(z + Z - 1))

    core_at = pl.multiple_of(core * FC, FC)
    other_at = pl.multiple_of((1 - core) * FC, FC)

    count = [0, 0]
    sent = [None] * SENDS

    def slot(n=1):
        count[0] += n
        return count[0] - n

    def send(src, dst, device, to=None):
        at = count[1] % SENDS
        count[1] += 1
        if sent[at] is not None:
            sent[at].wait_send()
        copy = pltpu.make_async_remote_copy(
            src_ref=src, dst_ref=dst, send_sem=send_sem.at[at],
            recv_sem=recv_sem.at[slot() if to is None else to],
            device_id=device, device_id_type=MESH,
        )
        copy.start()
        sent[at] = copy
        return copy

    def arrived(ref, at):
        pltpu.make_async_remote_copy(
            src_ref=ref, dst_ref=ref, send_sem=send_sem.at[0], recv_sem=recv_sem.at[at],
            device_id=sibling, device_id_type=MESH,
        ).wait_recv()

    own_f = pl.multiple_of(y * FQ, FQ)
    near_f = [pl.multiple_of(((y + 1) % 4) * FQ, FQ), pl.multiple_of(((y + 3) % 4) * FQ, FQ)]
    loads = []

    def load(src, dst):
        copy = pltpu.make_async_copy(src, dst, load_sem.at[len(loads)])
        copy.start()
        loads.append(copy)

    for way in range(2):
        load(wu.at[:, pl.ds(near_f[way], FQ)], raw_un.at[way])
        load(wd.at[pl.ds(near_f[way], FQ), :], raw_dn.at[way])
    load(wu.at[:, pl.ds(own_f, FQ)], raw_u)
    load(wd.at[pl.ds(own_f, FQ), :], raw_d)

    barrier = pltpu.get_barrier_semaphore()
    greeted = [sibling, *z_next]
    greeted += [at_y(y + d, k) for d in (1, 2, 3) for k in (0, 1)]
    greeted += [at_x(x + d, k) for d in (1, 2, 3) for k in (0, 1)]
    for other in greeted:
        pl.semaphore_signal(barrier, inc=1, device_id=other, device_id_type=MESH)

    def block(xv, r, p, half):
        at = pl.multiple_of(p * 512 + (xv % 4) * 128 + r * ROWS, ROWS)
        return x_all.at[pl.ds(at, ROWS), pl.ds(pl.multiple_of(half * DW, DW), DW)]

    stage[0] = tok[...]
    stage[1] = grad[...]
    own_rows = pl.multiple_of(dp * 512 + row * ROWS, ROWS)
    x_all[pl.ds(own_rows, ROWS), 0:DW] = stage[core]
    pl.semaphore_wait(barrier, len(greeted))

    swap = send(stage.at[1 - core], block(x, core, dp, 0), sibling)
    first_trip = {}
    for d in (1, 3, 2):
        base = slot(2)
        first_trip[d] = base
        to_x, to_y = (x + core * d) % 4, (y + (1 - core) * d) % 4
        for arr in range(2):
            send(
                stage.at[arr],
                block(x, core, dp, (1 - core) * (d % 2)),
                {"row": to_x * 2 + arr, "col": (to_y % 2) * Z + z, "dp": to_y // 2},
                base + core,
            )
    repeat_masks(mask_up, mask_down, ku, kd)

    def trip_in(d):
        for r in range(2):
            arrived(block(x, r, dp, 0), first_trip[d] + r)

    before, after = ((y + 3) % 4) // 2, ((y + 1) % 4) // 2
    near_x, near_y, onward = {}, {}, []

    def send_x(name, p, half):
        near_x[name] = [
            send(block(x, 0, p, half), block(x, 0, p, half), x_next[way]) for way in range(2)
        ]

    def send_y(d):
        near_y[d] = [
            send(block(x + d, 1, dp, 0), block(x + d, 1, dp, 1), y_next[way]) for way in range(2)
        ]

    def on_x(name, p, half, way):
        for copy in near_x[name]:
            copy.wait_recv()
        there = x + 3 if way == 0 else x + 1
        onward.append(send(block(there, 0, p, half), block(there, 0, p, half), x_next[way]))

    def on_y(d, way):
        for copy in near_y[d]:
            copy.wait_recv()
        p = before if way == 0 else after
        onward.append(send(block(x + d, 1, p, 1), block(x + d, 1, p, 0), y_next[way]))

    near_slots = {}

    def near_weights(c):
        for way in range(2):
            f_at = c * FC + way * 128
            for i in range(6):
                keep = ku[i : i + 1, pl.ds(near_f[way] + f_at, 128)]
                w_near[c, way, 0, i * 64 : i * 64 + 64, :] = (
                    raw_un[way, i * 64 : i * 64 + 64, f_at : f_at + 128].astype(F32) * keep
                ).astype(BF16)
            rows = []
            for i in range(2):
                keep = kd[pl.ds(near_f[way] // 64 + f_at // 64 + i, 1), :]
                rows.append(raw_dn[way, f_at + i * 64 : f_at + i * 64 + 64, :].astype(F32) * keep)
            w_near[c, way, 1] = jnp.concatenate(rows, 0).T.astype(BF16)

    def send_weights(c):
        for way in range(2):
            base = slot(2)
            near_slots[c, way] = base
            for arr in range(2):
                send(
                    w_near.at[c, way, arr],
                    w_all.at[c, pl.ds(DW, DW), pl.ds(core_at + way * 128, 128)],
                    at_y(y + (1 if way == 0 else 3), arr),
                    base + core,
                )

    own_in = {}

    def own_weights(c):
        for i in range(6):
            keep = ku[i : i + 1, pl.ds(own_f + c * FC, FC)]
            w_own[c, 0, i * 64 : i * 64 + 64, :] = (
                raw_u[i * 64 : i * 64 + 64, c * FC : (c + 1) * FC].astype(F32) * keep
            ).astype(BF16)
        rows = []
        for i in range(FC // 64):
            at = c * FC + i * 64
            keep = kd[pl.ds(own_f // 64 + at // 64, 1), :]
            rows.append(raw_d[at : at + 64, :].astype(F32) * keep)
        w_own[c, 1] = jnp.concatenate(rows, 0).T.astype(BF16)
        own_in[c] = send(
            w_own.at[c, 1 - core], w_all.at[c, pl.ds(0, DW), pl.ds(core_at, FC)], sibling
        )
        w_all[c, 0:DW, pl.ds(core_at, FC)] = w_own[c, core]

    def weights_in(c):
        own_in[c].wait_recv()
        for way in range(2):
            for r in range(2):
                arrived(
                    w_all.at[c, pl.ds(DW, DW), pl.ds(r * FC + way * 128, 128)], near_slots[c, way] + r
                )

    swap.wait_recv()
    send_x("own", dp, 0)
    send_y(0)
    for copy in loads[:4]:
        copy.wait()
    near_weights(0)
    send_weights(0)
    trip_in(1)
    trip_in(3)
    send_x("after", after, 1)
    send_x("before", before, 1)
    send_y(1)
    send_y(3)
    trip_in(2)
    send_x("far", 1 - dp, 0)
    send_y(2)
    on_x("own", dp, 0, 0)
    on_y(0, 0)
    for copy in loads[4:]:
        copy.wait()
    own_weights(0)
    near_weights(1)
    on_x("after", after, 1, 0)
    on_y(1, 0)
    on_x("before", before, 1, 1)
    on_y(3, 1)
    on_x("far", 1 - dp, 0, 1)
    on_y(2, 1)
    send_weights(1)
    own_weights(1)
    near_weights(2)
    send_weights(2)
    own_weights(2)
    for copy in onward:
        copy.wait_recv()

    def steps_of(r, way):
        return 4 if r == way else 3

    def rows_of(j):
        return pl.ds(pl.multiple_of((j % Z) * TB, TB), TB)

    def pre_part(c):
        weights_in(c)

        def body(i, carry):
            rows = pl.ds(pl.multiple_of(i * 256, 256), 256)
            part[c, rows, :] = dot_nn(x_all[rows, :], w_all[c])
            return carry

        lax.fori_loop(0, TOK // 256, body, 0)

    def pre_block(c, j):
        part[c, rows_of(j), :] = dot_nn(x_all[rows_of(j), :], w_all[c])

    ring = {}
    half = [slice(0, FC), slice(FC, F2)]

    def reduce_step(c, s):
        for way in range(2):
            if s > 0:
                ring[c, way, s - 1].wait_recv()
            src = came.at[c, way, s - 1] if s > 0 else first.at[c, way]
            for r in range(2):
                n = steps_of(r, way)
                if s >= n:
                    continue
                dest = z + (n - s) if way == 0 else z + Z - (n - s)
                term = part[c, rows_of(dest), half[r]]
                if s > 0:
                    term = src[:, half[r]].astype(F32) + term
                src[:, half[r]] = term.astype(BF16)
            dst = came.at[c, way, s]
            if s == 3:
                src, dst = src.at[:, pl.ds(way * FC, FC)], dst.at[:, pl.ds(way * FC, FC)]
            ring[c, way, s] = send(src, dst, z_next[way])

    swaps = {}

    def finish(c):
        for way in range(2):
            ring[c, way, 3].wait_recv()
        for r in range(2):
            value = part[c, rows_of(z), half[r]]
            for way in range(2):
                value = value + came[c, way, steps_of(r, way) - 1, :, half[r]].astype(F32)
            swap_s[c, :, half[r]] = value
        swaps[c] = send(swap_s.at[c], swap_r.at[c], sibling)

    gather = {}

    def activate(c):
        swaps[c].wait_recv()
        mine, theirs = swap_s[c], swap_r[c]
        pre_act = jnp.where(core == 0, mine, theirs)
        grad_hidden = jnp.where(core == 0, theirs, mine)
        activated, slope = gelu_pair(pre_act)
        value = jnp.where(core == 0, grad_hidden * slope, activated)
        hid[c, rows_of(z), :] = value.astype(BF16)

    def gather_step(c, s):
        if s > 0:
            for way in range(2):
                gather[c, way, s - 1].wait_recv()
        for way in range(2):
            source = z + Z - s if way == 0 else z + s
            lanes = pl.ds(0, F2) if s < 3 else pl.ds(way * FC, FC)
            block_of = hid.at[c, rows_of(source), lanes]
            gather[c, way, s] = send(block_of, block_of, z_next[way])

    def gather_end(c):
        for way in range(2):
            gather[c, way, 3].wait_recv()

    def turn_tokens():
        for i in range(8):
            x_turned[:, i * 128 : i * 128 + 128] = x_all[i * 128 : i * 128 + 128, :].T

    def turn_weights(c):
        w_turned[c] = w_all[c].T

    scale = float(TOK) ** -0.5
    grads_in = {}

    def weight_grads(c):
        def width(dst, first_row):
            def body(i, carry):
                rows = pl.ds(pl.multiple_of(i * 128, 128), 128)
                wide = pl.ds(pl.multiple_of(first_row + i * 128, 128), 128)
                dst[c, rows, :] = (dot_nn(x_turned[wide, :], hid[c]) * scale).astype(BF16)
                return carry

            lax.fori_loop(0, DW // 128, body, 0)

        width(g_far, DW)
        base = slot(2)
        for r in range(2):
            send(
                g_far.at[c, :, pl.ds(r * FC, FC)], g_far_in.at[core, c],
                at_y(y + 1 - 2 * yl, r), base + core,
            )
        width(g_own, 0)
        across = send(g_own.at[c, :, pl.ds(other_at, FC)], g_sib.at[c], sibling)
        grads_in[c] = (across, base)

    def place(c, which, up, down):
        there = pl.multiple_of(which * FQ + c * FC, FC)
        mine = pl.multiple_of(dp * 2 * FQ + which * FQ + c * FC, FC)
        for i in range(6):
            keep = ku[i : i + 1, pl.ds(mine, FC)]
            gwu[i * 64 : i * 64 + 64, pl.ds(there, FC)] = (
                up[i * 64 : i * 64 + 64, :] * keep
            ).astype(BF16)
        down = down.T
        for i in range(FC // 64):
            keep = kd[pl.ds(mine // 64 + i, 1), :]
            gwd[pl.ds(there + i * 64, 64), :] = (down[i * 64 : i * 64 + 64, :] * keep).astype(BF16)

    def place_own(c):
        grads_in[c][0].wait_recv()
        own, sib = g_own[c, :, pl.ds(core_at, FC)].astype(F32), g_sib[c].astype(F32)
        place(c, yl, jnp.where(core == 0, own, sib), jnp.where(core == 0, sib, own))

    def place_far(c):
        for arr in range(2):
            arrived(g_far_in.at[arr, c], grads_in[c][1] + arr)
        place(c, 1 - yl, g_far_in[0, c].astype(F32), g_far_in[1, c].astype(F32))

    def act_part(c):
        def body(i, carry):
            rows = pl.ds(pl.multiple_of(i * 256, 256), 256)
            o = dot_nn(hid[c, rows, :], w_turned[c])
            acc[rows, :] = o if c == 0 else o + acc[rows, :]
            return carry

        lax.fori_loop(0, TOK // 256, body, 0)

    weights_in(0)
    for j in (z + 4, z + 3, z + 5):
        pre_block(0, j)
    reduce_step(0, 0)
    for j in (z + 2, z + 6, z + 1, z + 7, z):
        pre_block(0, j)
    pre_part(1)
    reduce_step(1, 0)
    reduce_step(0, 1)
    turn_tokens()
    reduce_step(1, 1)
    reduce_step(0, 2)
    pre_part(2)
    reduce_step(2, 0)
    turn_weights(0)
    reduce_step(0, 3)
    reduce_step(1, 2)
    reduce_step(2, 1)
    finish(0)
    turn_weights(1)
    activate(0)
    gather_step(0, 0)
    reduce_step(1, 3)
    reduce_step(2, 2)
    gather_step(0, 1)
    finish(1)
    turn_weights(2)
    reduce_step(2, 3)
    activate(1)
    gather_step(1, 0)
    gather_step(0, 2)
    finish(2)
    activate(2)
    gather_step(2, 0)
    gather_step(0, 3)
    gather_step(1, 1)
    gather_step(2, 1)
    gather_step(1, 2)
    gather_end(0)
    weight_grads(0)
    gather_step(2, 2)
    gather_step(1, 3)
    act_part(0)
    gather_step(2, 3)
    gather_end(1)
    weight_grads(1)
    gather_end(2)

    def x_rows(xv, p):
        return pl.ds(pl.multiple_of(p * 512 + (xv % 4) * 128, 128), 128)

    def x_first(xv, p):
        rows = x_rows(xv, p)
        late = dot_nn(hid[1, rows, :], w_turned[1]) + dot_nn(hid[2, rows, :], w_turned[2])
        return acc[rows, :] + late

    def x_term(xv, p):
        return acc[x_rows(xv, p), :]

    def x_send(at, value, way):
        xs[at] = value.astype(BF16)
        return send(xs.at[at], xr.at[at], x_next[way])

    r0 = x_send(0, x_first(x + 2, 0), 0)
    l0 = x_send(1, x_first(x + 2, 1), 1)
    r1b = x_send(2, x_first(x + 1, 1), 0)
    l1a = x_send(3, x_first(x + 3, 0), 1)
    for xv, p in ((x + 1, 0), (x + 3, 1), (x, 0), (x, 1)):
        acc[x_rows(xv, p), :] = x_first(xv, p)
    weight_grads(2)
    place_own(0)
    r0.wait_recv()
    r1a = x_send(4, x_term(x + 1, 0) + xr[0].astype(F32), 0)
    l0.wait_recv()
    l1b = x_send(5, x_term(x + 3, 1) + xr[1].astype(F32), 1)
    place_far(0)
    place_own(1)
    place_own(2)
    for copy in (r1b, l1a, r1a, l1b):
        copy.wait_recv()
    yfull[0:128, :] = x_term(x, 0) + xr[4].astype(F32) + xr[3].astype(F32)
    yfull[128:256, :] = x_term(x, 1) + xr[2].astype(F32) + xr[5].astype(F32)

    def y_term(half, r, p):
        at = pl.multiple_of(p * 128 + r * ROWS, ROWS)
        return yfull[pl.ds(at, ROWS), half * DW : half * DW + DW].astype(BF16)

    last = []
    for d, half, p in ((2, 0, 1 - dp), (1, 1, after), (3, 1, before)):
        base = slot(2)
        last.append((d, base))
        for r in range(2):
            ys[d, r] = y_term(half, r, p)
            send(ys.at[d, r], yr.at[core, d], at_y(y + d, r), base + core)
    ys[0, 0] = y_term(0, 1 - core, dp)
    across = send(ys.at[0, 0], yr.at[core, 0], sibling)
    yr[core, 0] = y_term(0, core, dp)
    place_far(1)
    place_far(2)
    for d, base in last:
        for arr in range(2):
            arrived(yr.at[arr, d], base + arr)
    across.wait_recv()
    for arr in range(2):
        total = yr[arr, 0].astype(F32) + yr[arr, 1].astype(F32) + yr[arr, 2].astype(F32)
        acts[arr] = (total + yr[arr, 3].astype(F32)).astype(BF16)

    for copy in sent:
        if copy is not None:
            copy.wait_send()


def place_kernel(acts, gwu, gwd, out, gin, gwu_out, gwd_out):
    gin[...] = acts[0]
    out[...] = acts[1]
    gwu_out[...] = gwu[...]
    gwd_out[...] = gwd[...]


def local(tokens, grad_out, w_up, w_down, mask_up, mask_down):
    vmem = pl.BlockSpec(memory_space=pltpu.VMEM)
    hbm = pl.BlockSpec(memory_space=pl.ANY)
    keeps = [pltpu.VMEM((6, 4 * FQ), F32), pltpu.VMEM((48, DW), F32)]
    acts, grad_up, grad_down = pl.pallas_call(
        kernel,
        out_shape=(
            jax.ShapeDtypeStruct((2, ROWS, DW), BF16),
            jax.ShapeDtypeStruct((DW, 2 * FQ), BF16),
            jax.ShapeDtypeStruct((2 * FQ, DW), BF16),
        ),
        in_specs=[vmem, vmem, hbm, hbm, vmem, vmem],
        out_specs=(vmem, vmem, vmem),
        scratch_shapes=[
            *keeps,
            pltpu.VMEM((2, ROWS, DW), BF16),
            pltpu.VMEM((TOK, D2), BF16),
            pltpu.VMEM((D2, TOK), BF16),
            pltpu.VMEM((DW, FQ), BF16),
            pltpu.VMEM((2, DW, FQ), BF16),
            pltpu.VMEM((FQ, DW), BF16),
            pltpu.VMEM((2, FQ, DW), BF16),
            pltpu.VMEM((C, D2, F2), BF16),
            pltpu.VMEM((C, F2, D2), BF16),
            pltpu.VMEM((C, 2, DW, FC), BF16),
            pltpu.VMEM((C, 2, 2, DW, 128), BF16),
            pltpu.VMEM((C, TOK, F2), F32),
            pltpu.VMEM((C, 2, TB, F2), BF16),
            pltpu.VMEM((C, 2, 4, TB, F2), BF16),
            pltpu.VMEM((C, TB, F2), F32),
            pltpu.VMEM((C, TB, F2), F32),
            pltpu.VMEM((C, TOK, F2), BF16),
            pltpu.VMEM((TOK, D2), F32),
            pltpu.VMEM((6, 128, D2), BF16),
            pltpu.VMEM((6, 128, D2), BF16),
            pltpu.VMEM((256, D2), F32),
            pltpu.VMEM((4, 2, ROWS, DW), BF16),
            pltpu.VMEM((2, 4, ROWS, DW), BF16),
            pltpu.VMEM((C, DW, F2), BF16),
            pltpu.VMEM((C, DW, F2), BF16),
            pltpu.VMEM((C, DW, FC), BF16),
            pltpu.VMEM((2, C, DW, FC), BF16),
            pltpu.SemaphoreType.DMA((8,)),
            pltpu.SemaphoreType.DMA((SENDS,)),
            pltpu.SemaphoreType.DMA((MESSAGES,)),
        ],
        compiler_params=pltpu.CompilerParams(
            collective_id=0, has_side_effects=True, vmem_limit_bytes=56 * 1024 * 1024
        ),
        cost_estimate=pl.CostEstimate(
            flops=12 * TOK * D2 * FQ, bytes_accessed=8 * 1024 * 1024, transcendentals=TB * FQ
        ),
    )(tokens, grad_out, w_up, w_down, mask_up, mask_down.T)
    return pl.pallas_call(
        place_kernel,
        out_shape=(
            jax.ShapeDtypeStruct((ROWS, DW), BF16),
            jax.ShapeDtypeStruct((ROWS, DW), BF16),
            jax.ShapeDtypeStruct((DW, 2 * FQ), BF16),
            jax.ShapeDtypeStruct((2 * FQ, DW), BF16),
        ),
        in_specs=[vmem] * 3,
        out_specs=(vmem,) * 4,
        compiler_params=pltpu.CompilerParams(vmem_limit_bytes=60 * 1024 * 1024),
    )(acts, grad_up, grad_down)


def solution(mesh):
    in_specs = (
        P(("row", "dp"), "col"),
        P(("row", "dp"), "col"),
        P("col", "row"),
        P("row", "col"),
        P("col", "row"),
        P("row", "col"),
    )
    out_specs = (
        P(("row", "dp"), "col"),
        P(("row", "dp"), "col"),
        P("col", ("row", "dp")),
        P(("row", "dp"), "col"),
    )
    return jax.shard_map(local, mesh=mesh, in_specs=in_specs, out_specs=out_specs, check_vma=False)
```
